512 devices in a mesh: group: 8 (over x, core), member: 64 (over y, z).
Axes of the slice: x: 4, y: 8, z: 8, core: 2. Of those that a mesh axis runs over, the one named last changes fastest.
Arguments:
- queries: bfloat16 [24576, 4096], P(('group', 'member')), may hold values from -48 to 48
- passages: bfloat16 [2048, 4096], P(('group', 'member')), may hold values from -6 to 6
- pool: bfloat16 [65536, 4096], P(('group', 'member')), may hold values from -6 to 6
- positives: int32 [24576], P(('group', 'member')), may hold values from 0 to 255
- weights: float32 [24576], P(('group', 'member')), may hold values from 4 to 64
- requests: int32 [512, 8], P(('group', 'member')), may hold values from 0 to 1, as said below
Outputs:
- grad_queries: bfloat16 [24576, 4096], P(('group', 'member'))
- grad_passages: bfloat16 [2048, 4096], P(('group', 'member'))
- grad_pool: bfloat16 [65536, 4096], P(('group', 'member'))
The draws below stay inside these ranges and needn't reach their ends.
Inputs may be any that keep to these rules, and one draw needn't show every extreme that they name: `requests`: 0 in the column of the block's own group.
All inputs are finite; a program needn't handle non-finite values.
Results may differ from the reference program's by a relative error of at most 0.0065.
Values may be sent and summed in bfloat16 or wider, within the bound.
A program may use at most 64 MiB of HBM per device.

```python
import math
import jax
import jax.numpy as jnp

D = 4096
Q_DEV = 48
P_DEV = 4
HB = 128
GROUPS = 8
MEMBERS = 64
BLOCKS = 512
PG = 256
QN = 24576
PN = 2048
HN = 65536
N_MEMBER = 64


def shared_passages(key):
    values = jax.random.normal(key, (PN, D), jnp.float32)
    return jnp.clip(values, -6.0, 6.0)


def draw_passages(key, part):
    shared = shared_passages(key)
    return shared.astype(jnp.bfloat16)


def draw_queries(key, part):
    key = jax.random.fold_in(key, 12)
    values = jnp.clip(jax.random.normal(key, (QN, D), jnp.float32), -6.0, 6.0)
    return values.astype(jnp.bfloat16)


def draw_requests(key, part):
    key = jax.random.fold_in(key, 13)
    appeal_key, dice_key = jax.random.split(key)
    appeal = jax.random.randint(appeal_key, (GROUPS,), 1, 9)
    dice_rolls = jax.random.randint(dice_key, (BLOCKS, GROUPS), 0, 8)
    own_group = jnp.arange(BLOCKS, dtype=jnp.int32) // MEMBERS
    foreign = jnp.arange(GROUPS, dtype=jnp.int32)[None, :] != own_group[:, None]
    return ((dice_rolls < appeal[None, :]) & foreign).astype(jnp.int32)


def place_ends(entries, key, low, top_value):
    extent = entries.shape
    spot = [jax.random.randint(jax.random.fold_in(key, axis), (), 0, extent[axis]) for axis in range(len(extent))]
    entries = entries.at[tuple(spot)].set(low)
    longest = extent.index(max(extent))
    spot[longest] = (spot[longest] + 1) % extent[longest]
    return entries.at[tuple(spot)].set(top_value)


def steps_of(stream_key, shape, cuts, low, top_value):
    factor_of, own = 1.0, jax.random.fold_in(stream_key, 6)
    for dim, parts in cuts:
        draws = jnp.exp(jax.random.uniform(jax.random.fold_in(own, dim), (parts,), jnp.float32, low / len(cuts), top_value / len(cuts)))
        factor_of = factor_of * jnp.repeat(draws, shape[dim] // parts).reshape([-1 if axis == dim else 1 for axis in range(len(shape))])
    return factor_of


def bell_draw(key, dims, spread, limit, cuts=(), kind=jnp.bfloat16):
    array = jax.random.normal(key, dims, jnp.float32) * spread
    if len(cuts) > 0:
        array = steps_of(key, dims, cuts, -0.22, 0.18) * array
    return jnp.clip(array, min=-limit, max=limit).astype(kind)


def setup_inputs(seed: int = 0) -> dict:
    splits = jax.random.split(jax.random.key(seed), 7)
    return {
        "queries": draw_queries(jax.random.fold_in(splits[6], 71), 0),
        "passages": draw_passages(jax.random.fold_in(splits[6], 71), 0),
        "pool": bell_draw(splits[2], (HN, D), 1.0, 6.0, ((0, 512),)),
        "positives": place_ends(jax.random.randint(splits[3], (QN,), 0, P_DEV * N_MEMBER), jax.random.fold_in(splits[3], 1), 0, (P_DEV * N_MEMBER) - 1).astype(jnp.int32),
        "weights": jnp.clip(jnp.exp(math.log(64.0) - 2.7725887 * jax.random.uniform(splits[4], (QN,), jnp.float32) ** steps_of(splits[4], (QN,), ((0, 512),), -0.2, 0.2)), 4.0, 64.0),
        "requests": draw_requests(jax.random.fold_in(splits[6], 71), 0),
    }


def reference(queries, passages, pool, positives, weights, requests):
    factor = D ** -0.5
    query_grid = queries.reshape(GROUPS, MEMBERS, Q_DEV, D).astype(jnp.float32)
    batch_grid = passages.reshape(GROUPS, PG, D).astype(jnp.float32)
    pool_grid = pool.reshape(GROUPS, MEMBERS, HB, D).astype(jnp.float32)
    wanted = (requests.reshape(GROUPS, MEMBERS, GROUPS) != 0)[:, :, :, None, None]
    in_scores = jnp.einsum("gmqd,gpd->gmqp", query_grid, batch_grid) * factor
    hard_scores = jnp.einsum("gmqd,omhd->gmoqh", query_grid, pool_grid) * factor
    hard_scores = jnp.where(wanted, hard_scores, -1e30)
    highest = jnp.maximum(jnp.max(in_scores, axis=3), jnp.max(hard_scores, axis=(2, 4)))
    totals = jnp.sum(jnp.exp(in_scores - highest[..., None]), axis=3)
    totals = totals + jnp.sum(jnp.exp(hard_scores - highest[:, :, None, :, None]), axis=(2, 4))
    logsum = highest + jnp.log(totals)
    loss_weights = weights.reshape(GROUPS, MEMBERS, Q_DEV)
    targets = positives.reshape(GROUPS, MEMBERS, Q_DEV)
    one_hot = (jnp.arange(PG).astype(jnp.int32)[None, None, None, :] == targets[..., None]).astype(jnp.float32)
    in_coefs = (loss_weights[..., None] * (jnp.exp(in_scores - logsum[..., None]) - one_hot) * factor).astype(jnp.bfloat16)
    hard_coefs = (loss_weights[:, :, None, :, None] * jnp.exp(hard_scores - logsum[:, :, None, :, None]) * factor).astype(jnp.bfloat16)
    in_wide = in_coefs.astype(jnp.float32)
    hard_wide = hard_coefs.astype(jnp.float32)
    grad_queries = jnp.einsum("gmqp,gpd->gmqd", in_wide, batch_grid) + jnp.einsum("gmoqh,omhd->gmqd", hard_wide, pool_grid)
    grad_passages = jnp.einsum("gmqp,gmqd->gpd", in_wide, query_grid)
    grad_pool = jnp.einsum("gmoqh,gmqd->omhd", hard_wide, query_grid)
    return (grad_queries.reshape(queries.shape).astype(jnp.bfloat16),
            grad_passages.reshape(passages.shape).astype(jnp.bfloat16),
            grad_pool.reshape(pool.shape).astype(jnp.bfloat16))
```

```python
import functools

import jax
import jax.numpy as jnp
from jax import lax
from jax.experimental import pallas as pl
from jax.experimental.pallas import tpu as pltpu
from jax.sharding import PartitionSpec as P

MESH = pl.DeviceIdType.MESH
F32 = jnp.float32
BF16 = jnp.bfloat16

D = 4096
Q = 48
HB = 128
W = 1024
HW = 512
QW = 256
HALF = D // 2
N = 8
HOPS = N // 2
FACTOR = D ** (-0.5)
NEG = -1e30


def nt(a, b):
    return lax.dot_general(a, b, (((1,), (1,)), ((), ())), preferred_element_type=F32)


def nn(a, b):
    return lax.dot_general(a, b, (((1,), (0,)), ((), ())), preferred_element_type=F32)


def tn(a, b):
    return lax.dot_general(a, b, (((0,), (0,)), ((), ())), preferred_element_type=F32)


def loop(n, body):
    lax.fori_loop(0, n, lambda i, _: (body(i), 0)[1], 0)


def cols(i, size):
    return pl.ds(pl.multiple_of(i * size, size), size)


def kernel(
    q_ref, p_ref, pool_ref, pos_ref, w_ref, req_ref,
    gq_ref, gp_ref, gpool_ref,
    q_all, pool2, ga, gb, meta, sc, pb, part, fw, rx, st_out, st, sto, ls,
    q4, tin, cin, gpa, gpb, ra, rb, rah, rbh, sa, sb, sa_in, sb_in,
    gq_acc, gq_out, cb, gpo_out, gpo_in, gpo_acc, gpo_done, gp_done,
    loc, qs, qr, ps, pr, ms, mr, a1s, a1r, b1s, b1r, ags, agr, sts, str_, lss, lsr,
    pts, ptr, gps, gpr, rss, rsr, a2s, a2r, b2s, b2r,
):
    g = lax.axis_index("group")
    mem = lax.axis_index("member")
    x, c = lax.div(g, 2), lax.rem(g, 2)
    y, z = lax.div(mem, N), lax.rem(mem, N)
    right = (lax.rem(x + 1, 4) * 2 + c, mem)
    left = (lax.rem(x + 3, 4) * 2 + c, mem)
    opp = (lax.rem(x + 2, 4) * 2 + c, mem)
    mate_group = x * 2 + 1 - c
    mate = (mate_group, mem)

    def yd(d):
        return (g, lax.rem(y + d, N) * N + z)

    def zd(d):
        return (g, y * N + lax.rem(z + d, N))

    def rc(src, dst, ssem, rsem, dev):
        return pltpu.make_async_remote_copy(
            src_ref=src, dst_ref=dst, send_sem=ssem, recv_sem=rsem,
            device_id=dev, device_id_type=MESH,
        )

    sent = []

    def go(copy):
        copy.start()
        sent.append(copy)

    barrier = pltpu.get_barrier_semaphore()
    for dev in (right, left, opp, mate):
        pl.semaphore_signal(barrier, inc=1, device_id=dev, device_id_type=MESH)
    for d in range(1, N):
        pl.semaphore_signal(barrier, inc=1, device_id=yd(d), device_id_type=MESH)
        pl.semaphore_signal(barrier, inc=1, device_id=zd(d), device_id_type=MESH)

    load_q = pltpu.make_async_copy(q_ref, q_all.at[0], loc.at[0])
    load_pool = pltpu.make_async_copy(pool_ref, pool2.at[pl.ds(0, HB)], loc.at[1])
    load_q.start()
    load_pool.start()

    pf = p_ref[...].astype(F32)
    row16 = lax.broadcasted_iota(jnp.int32, (16, HW), 0)

    def fold(off):
        acc = jnp.zeros((16, HW), F32)
        for r in range(4):
            for k in range(4):
                piece = pf[r:r + 1, k * W + off:k * W + off + HW]
                acc = jnp.where(row16 == 4 * r + k, piece, acc)
        return acc.astype(BF16)

    ga[y, z] = fold(0)
    gb[y, z] = fold(HW)
    meta[0] = jnp.zeros((8, 128), F32)
    meta[0, 0:1, 0:8] = req_ref[...].astype(F32)

    pl.semaphore_wait(barrier, 4 + 2 * (N - 1))

    for d in range(1, N):
        go(rc(ga.at[y, z], ga.at[y, z], a1s.at[d], a1r.at[d], zd(d)))
        go(rc(gb.at[y, z], gb.at[y, z], b1s.at[d], b1r.at[d], yd(d)))
    h0, h1 = pl.ds(0, HALF), pl.ds(HALF, HALF)
    go(rc(q_ref.at[:, h0], q_all.at[1, :, h0], qs.at[0], qr.at[0], right))
    go(rc(q_ref.at[:, h1], q_all.at[2, :, h1], qs.at[2], qr.at[2], left))
    go(rc(meta.at[0], meta.at[1], ms.at[0], mr.at[0], right))
    go(rc(meta.at[0], meta.at[2], ms.at[1], mr.at[1], left))
    go(rc(meta.at[0], meta.at[3], ms.at[2], mr.at[2], opp))
    go(rc(pool_ref, pool2.at[pl.ds(HB, HB)], ps.at[0], pr.at[0], mate))
    go(rc(q_ref.at[:, h1], q_all.at[1, :, h1], qs.at[1], qr.at[1], right))
    go(rc(q_ref.at[:, h0], q_all.at[2, :, h0], qs.at[3], qr.at[3], left))

    def arrived(ref, sem):
        rc(ref, ref, sem, sem, right).wait_recv()

    def ring(flow, d):
        sign = 1 if flow % 2 == 0 else -1
        if flow < 2:
            blk = lax.rem(y - sign * d + N, N)
            if d == HOPS:
                return ga.at[blk, :, :, pl.ds(0 if sign > 0 else QW, QW)]
            return ga.at[blk]
        blk = lax.rem(z - sign * d + N, N)
        if d == HOPS:
            return gb.at[:, blk, :, pl.ds(0 if sign > 0 else QW, QW)]
        return gb.at[:, blk]

    def ring_send(d):
        for flow in range(4):
            sign = 1 if flow % 2 == 0 else -1
            if flow < 2:
                blk = lax.rem(y - sign * (d - 1) + N, N)
                src = ga.at[blk]
                if d == HOPS:
                    src = ga.at[blk, :, :, pl.ds(0 if sign > 0 else QW, QW)]
                dev = yd(1 if sign > 0 else N - 1)
            else:
                blk = lax.rem(z - sign * (d - 1) + N, N)
                src = gb.at[:, blk]
                if d == HOPS:
                    src = gb.at[:, blk, :, pl.ds(0 if sign > 0 else QW, QW)]
                dev = zd(1 if sign > 0 else N - 1)
            if d > 1:
                arrived(ring(flow, d - 1), agr.at[flow, d - 2])
            go(rc(src, src, ags.at[flow, d - 1], agr.at[flow, d - 1], dev))

    for d in range(1, N):
        src = lax.rem(z + N - d, N)
        arrived(ga.at[y, src], a1r.at[d])
        src = lax.rem(y + N - d, N)
        arrived(gb.at[src, z], b1r.at[d])
    ring_send(1)

    lane256 = lax.broadcasted_iota(jnp.int32, (1, 2 * HB), 1)
    lane128 = lax.broadcasted_iota(jnp.int32, (1, 128), 1)

    def hard(slot):
        def body(i, acc):
            at = cols(i, 1024)
            return acc + nt(q_all[slot, :, at], pool2[:, at])

        scores = lax.fori_loop(0, 4, body, jnp.zeros((Q, 2 * HB), F32)) * FACTOR
        line = meta[slot, 0:1, :]
        here = jnp.sum(jnp.where(lane128 == g, line, 0.0), axis=1, keepdims=True)
        there = jnp.sum(jnp.where(lane128 == mate_group, line, 0.0), axis=1, keepdims=True)
        asked = jnp.where(lane256 < HB, here, there) != 0.0
        scores = jnp.where(asked, scores, NEG)
        sc[slot] = scores
        top = jnp.max(scores, axis=1, keepdims=True)
        probs = jnp.where(asked, jnp.exp(scores - top), 0.0)
        total = jnp.sum(probs, axis=1, keepdims=True)
        pb[slot] = probs.astype(BF16)
        st_out[slot] = jnp.where(lane128 < 64, top, total)

    arrived(q_all.at[1, :, h0], qr.at[0])
    go(rc(q_all.at[1, :, h0], q_all.at[3, :, h0], qs.at[4], qr.at[4], right))
    arrived(q_all.at[2, :, h1], qr.at[2])
    go(rc(q_all.at[2, :, h1], q_all.at[3, :, h1], qs.at[5], qr.at[5], left))

    load_q.wait()
    load_pool.wait()
    arrived(pool2.at[pl.ds(HB, HB)], pr.at[0])
    hard(0)
    for k in range(4):
        q4[0, k * Q:(k + 1) * Q, :] = q_all[0, :, k * W:k * W + HW]
        q4[1, k * Q:(k + 1) * Q, :] = q_all[0, :, k * W + HW:(k + 1) * W]
    ring_send(2)

    arrived(q_all.at[1, :, h1], qr.at[1])
    arrived(meta.at[1], mr.at[0])
    hard(1)
    go(rc(st_out.at[1], st.at[2], sts.at[0], str_.at[0], left))
    arrived(q_all.at[2, :, h0], qr.at[3])
    arrived(meta.at[2], mr.at[1])
    hard(2)
    go(rc(st_out.at[2], st.at[1], sts.at[1], str_.at[1], right))
    ring_send(3)

    arrived(q_all.at[3, :, h0], qr.at[4])
    arrived(q_all.at[3, :, h1], qr.at[5])
    arrived(meta.at[3], mr.at[2])
    hard(3)
    go(rc(st_out.at[3], st.at[3], sts.at[2], str_.at[2], opp))
    go(rc(st_out.at[3], sto.at[0], sts.at[3], str_.at[3], right))
    go(rc(st_out.at[3], sto.at[1], sts.at[4], str_.at[4], left))

    def partial(slot, first):
        def body(i):
            at = cols(i + first, 512)
            part[slot, :, at] = nn(pb[slot], pool2[:, at]).astype(BF16)

        loop(4, body)

    partial(3, 0)
    go(rc(part.at[3, :, h0], fw.at[0], pts.at[0], ptr.at[0], right))
    partial(3, 4)
    go(rc(part.at[3, :, h1], fw.at[1], pts.at[1], ptr.at[1], left))
    ring_send(4)
    partial(1, 0)
    go(rc(part.at[1, :, h0], rx.at[1, :, h0], pts.at[2], ptr.at[2], left))
    partial(2, 4)
    go(rc(part.at[2, :, h1], rx.at[0, :, h1], pts.at[3], ptr.at[3], right))

    for flow in range(4):
        arrived(ring(flow, HOPS), agr.at[flow, HOPS - 1])
    mod4 = lax.rem(lane256, 4)

    def in_block(b):
        pa = ga[pl.ds(2 * b, 2)].reshape(256, HW)
        pbk = gb[pl.ds(2 * b, 2)].reshape(256, HW)
        s = nt(q4[0], pa) + nt(q4[1], pbk)
        t = jnp.where(mod4 == 0, s[0:Q], 0.0)
        for k in range(1, 4):
            t = jnp.where(mod4 == k, s[k * Q:(k + 1) * Q], t)
        t = t + jnp.where(lax.rem(mod4, 2) == 0, pltpu.roll(t, 255, 1), pltpu.roll(t, 1, 1))
        t = t + jnp.where(mod4 < 2, pltpu.roll(t, 254, 1), pltpu.roll(t, 2, 1))
        tin[:, cols(b, 256)] = t * FACTOR

    loop(4, in_block)

    for i in range(3):
        arrived(st.at[(2, 1, 3)[i]], str_.at[i])
    tops = [st_out[0][:, 0:1]] + [st[i][:, 0:1] for i in (1, 2, 3)]
    sums = [st_out[0][:, 64:65]] + [st[i][:, 64:65] for i in (1, 2, 3)]
    t_in = tin[...]
    in_top = jnp.max(t_in, axis=1, keepdims=True)
    highest = in_top
    for t in tops:
        highest = jnp.maximum(highest, t)
    lane1024 = lax.broadcasted_iota(jnp.int32, (1, W), 1)
    in_sum = jnp.sum(
        jnp.where(lax.rem(lane1024, 4) == 0, jnp.exp(t_in - highest), 0.0), axis=1, keepdims=True
    )
    totals = in_sum
    for t, s in zip(tops, sums):
        totals = totals + s * jnp.exp(t - highest)
    logsum = highest + jnp.log(totals)
    eye = lax.broadcasted_iota(jnp.int32, (Q, Q), 0) == lax.broadcasted_iota(jnp.int32, (Q, Q), 1)
    weight = jnp.sum(jnp.where(eye, w_ref[...], 0.0), axis=1, keepdims=True)
    positive = jnp.sum(jnp.where(eye, pos_ref[...], 0), axis=1, keepdims=True)
    ls[0] = jnp.where(lane128 < 64, logsum, weight)
    go(rc(ls.at[0], ls.at[1], lss.at[0], lsr.at[0], right))
    go(rc(ls.at[0], ls.at[2], lss.at[1], lsr.at[1], left))
    go(rc(ls.at[0], ls.at[3], lss.at[2], lsr.at[2], opp))

    one_hot = (lax.div(lane1024, 4) == positive).astype(F32)
    coefs = weight * (jnp.exp(t_in - logsum) - one_hot) * FACTOR
    for k in range(4):
        cin[k * Q:(k + 1) * Q, :] = jnp.where(lax.rem(lane1024, 4) == k, coefs, 0.0).astype(BF16)

    def gp_block(b):
        cc = cin[:, cols(b, 128)]
        gpa[b] = tn(cc, q4[0]).astype(BF16).reshape(N, 16, HW)
        gpb[b] = tn(cc, q4[1]).astype(BF16).reshape(N, 16, HW)

    loop(N, gp_block)

    def chunk(flow, d):
        sign = 1 if flow % 2 == 0 else -1
        if flow < 2:
            return gpa, lax.rem(z + sign * d + N, N), 1
        return gpb, lax.rem(y + sign * d + N, N), 0

    def rs_view(flow, d, half):
        ref, blk, axis = chunk(flow, d)
        at = pl.ds(0 if flow % 2 == 0 else QW, QW) if half else pl.ds(0, HW)
        return ref.at[:, blk, :, at] if axis == 1 else ref.at[blk, :, :, at]

    def rs_slot(flow, s):
        if s == 0:
            return (rah if flow < 2 else rbh).at[flow % 2]
        return (ra if flow < 2 else rb).at[flow % 2, s - 1]

    def rs_dev(flow):
        d = 1 if flow % 2 == 0 else N - 1
        return zd(d) if flow < 2 else yd(d)

    def rs_send(s):
        for flow in range(4):
            if s > 0:
                arrived(rs_slot(flow, s - 1), rsr.at[flow, s - 1])
                dst = rs_view(flow, HOPS - s, s == 1)
                dst[...] = dst[...] + rs_slot(flow, s - 1)[...]
            go(rc(
                rs_view(flow, HOPS - s, s == 0), rs_slot(flow, s),
                rss.at[flow, s], rsr.at[flow, s], rs_dev(flow),
            ))

    rs_send(0)

    def merge(slot, way, first, dest, sem):
        arrived(sto.at[way], str_.at[3 + way])
        arrived(fw.at[way], ptr.at[way])
        mine, theirs = st_out[slot][:, 0:1], sto[way][:, 0:1]
        most = jnp.maximum(mine, theirs)
        a, b = jnp.exp(mine - most), jnp.exp(theirs - most)

        def body(i):
            at = cols(i + first, 512)
            own = nn(pb[slot], pool2[:, at])
            part[slot, :, at] = (own * a + fw[way, :, cols(i, 512)].astype(F32) * b).astype(BF16)

        loop(4, body)
        half = pl.ds(first * 512, HALF)
        go(rc(part.at[slot, :, half], rx.at[way, :, half], pts.at[sem], ptr.at[sem], dest))

    merge(2, 0, 0, right, 4)
    merge(1, 1, 4, left, 5)

    rs_send(1)

    for i in range(3):
        arrived(ls.at[i + 1], lsr.at[i])
    for slot in range(4):
        lsum, wt = ls[slot][:, 0:1], ls[slot][:, 64:65]
        cb[slot * Q:(slot + 1) * Q, :] = (wt * jnp.exp(sc[slot] - lsum) * FACTOR).astype(BF16)

    def far_pool(i):
        at = cols(i, 512)
        gpo_out[:, at] = tn(cb[:, HB:2 * HB], q_all[:, :, at].reshape(4 * Q, 512)).astype(BF16)

    loop(8, far_pool)
    go(rc(gpo_out, gpo_in, gps.at[0], gpr.at[0], mate))

    rs_send(2)

    def near_pool(i):
        at = cols(i, 512)
        gpo_acc[:, at] = tn(cb[:, 0:HB], q_all[:, :, at].reshape(4 * Q, 512))

    loop(8, near_pool)

    rs_send(3)

    def own_rows(i):
        at = cols(i, 512)
        gq_acc[:, at] = nn(cb[0:Q, :], pool2[:, at])

    loop(8, own_rows)

    for flow in range(4):
        arrived(rs_slot(flow, HOPS - 1), rsr.at[flow, HOPS - 1])
    sa[...] = (
        gpa[:, z].astype(F32) + ra[0, HOPS - 2].astype(F32) + ra[1, HOPS - 2].astype(F32)
    ).astype(BF16)
    sb[...] = (
        gpb[y].astype(F32) + rb[0, HOPS - 2].astype(F32) + rb[1, HOPS - 2].astype(F32)
    ).astype(BF16)
    for d in range(1, N):
        go(rc(sa.at[lax.rem(y + d, N)], sa_in.at[d], a2s.at[d], a2r.at[d], yd(d)))
        go(rc(sb.at[lax.rem(z + d, N)], sb_in.at[d], b2s.at[d], b2r.at[d], zd(d)))

    for h, ref in ((0, ga), (1, gb)):
        for n in range(2):
            at = pl.ds(n * QW, QW)
            rows = nn(cin[...], ref[:, :, :, at].reshape(W, QW))
            for k in range(4):
                to = pl.ds(k * W + h * HW + n * QW, QW)
                gq_acc[:, to] = gq_acc[:, to] + rows[k * Q:(k + 1) * Q]

    arrived(gpo_in, gpr.at[0])

    def pool_sum(i):
        at = cols(i, 512)
        gpo_done[:, at] = (gpo_acc[:, at] + gpo_in[:, at].astype(F32)).astype(BF16)

    loop(8, pool_sum)
    store_pool = pltpu.make_async_copy(gpo_done, gpool_ref, loc.at[2])
    store_pool.start()

    scale = weight * FACTOR

    def back(t):
        return scale * jnp.exp(t - logsum)

    t_l, t_r, t_o = tops[1], tops[2], tops[3]
    arrived(rx.at[1, :, h0], ptr.at[2])
    arrived(rx.at[0, :, h1], ptr.at[3])
    arrived(rx.at[0, :, h0], ptr.at[4])
    arrived(rx.at[1, :, h1], ptr.at[5])

    def finish(first, e_l, e_r):
        def body(i):
            at = cols(i + first, 512)
            gq_out[:, at] = (
                gq_acc[:, at] + rx[0, :, at].astype(F32) * e_l + rx[1, :, at].astype(F32) * e_r
            ).astype(BF16)

        loop(4, body)

    finish(0, back(jnp.maximum(t_l, t_o)), back(t_r))
    finish(4, back(t_l), back(jnp.maximum(t_r, t_o)))
    store_q = pltpu.make_async_copy(gq_out, gq_ref, loc.at[3])
    store_q.start()

    row4 = lax.broadcasted_iota(jnp.int32, (4, HW), 0)
    for h, own, held, sem in ((0, sa[y], sa_in, a2r), (1, sb[z], sb_in, b2r)):
        acc = own.astype(F32)
        for d in range(1, N):
            arrived(held.at[d], sem.at[d])
            acc = acc + held[d].astype(F32)
        for k in range(4):
            out = jnp.zeros((4, HW), F32)
            for r in range(4):
                out = jnp.where(row4 == r, acc[4 * r + k:4 * r + k + 1, :], out)
            gp_done[:, k * W + h * HW:k * W + (h + 1) * HW] = out.astype(BF16)
    store_p = pltpu.make_async_copy(gp_done, gp_ref, loc.at[4])
    store_p.start()

    for copy in sent:
        copy.wait_send()
    store_pool.wait()
    store_q.wait()
    store_p.wait()


def per_device(queries, passages, pool, positives, weights, requests):
    dma = pltpu.SemaphoreType.DMA
    v = pltpu.VMEM
    scratch = [
        v((4, Q, D), BF16),
        v((2 * HB, D), BF16),
        v((N, N, 16, HW), BF16),
        v((N, N, 16, HW), BF16),
        v((4, 8, 128), F32),
        v((4, Q, 2 * HB), F32),
        v((4, Q, 2 * HB), BF16),
        v((4, Q, D), BF16),
        v((2, Q, HALF), BF16),
        v((2, Q, D), BF16),
        v((4, Q, 128), F32),
        v((4, Q, 128), F32),
        v((2, Q, 128), F32),
        v((4, Q, 128), F32),
        v((2, 4 * Q, HW), BF16),
        v((Q, W), F32),
        v((4 * Q, W), BF16),
        v((N, N, 16, HW), BF16),
        v((N, N, 16, HW), BF16),
        v((2, HOPS - 1, N, 16, HW), BF16),
        v((2, HOPS - 1, N, 16, HW), BF16),
        v((2, N, 16, QW), BF16),
        v((2, N, 16, QW), BF16),
        v((N, 16, HW), BF16),
        v((N, 16, HW), BF16),
        v((N, 16, HW), BF16),
        v((N, 16, HW), BF16),
        v((Q, D), F32),
        v((Q, D), BF16),
        v((4 * Q, 2 * HB), BF16),
        v((HB, D), BF16),
        v((HB, D), BF16),
        v((HB, D), F32),
        v((HB, D), BF16),
        v((4, D), BF16),
        dma((5,)),
        dma((6,)), dma((6,)),
        dma((1,)), dma((1,)),
        dma((3,)), dma((3,)),
        dma((N,)), dma((N,)), dma((N,)), dma((N,)),
        dma((4, HOPS)), dma((4, HOPS)),
        dma((5,)), dma((5,)),
        dma((3,)), dma((3,)),
        dma((6,)), dma((6,)),
        dma((1,)), dma((1,)),
        dma((4, HOPS)), dma((4, HOPS)),
        dma((N,)), dma((N,)), dma((N,)), dma((N,)),
    ]
    hbm = pl.BlockSpec(memory_space=pl.ANY)
    vmem = pl.BlockSpec(memory_space=pltpu.VMEM)
    return pl.pallas_call(
        kernel,
        out_shape=(
            jax.ShapeDtypeStruct((Q, D), BF16),
            jax.ShapeDtypeStruct((4, D), BF16),
            jax.ShapeDtypeStruct((HB, D), BF16),
        ),
        in_specs=[hbm, vmem, hbm, vmem, vmem, vmem],
        out_specs=(hbm, hbm, hbm),
        scratch_shapes=scratch,
        compiler_params=pltpu.CompilerParams(
            collective_id=0, has_side_effects=True, vmem_limit_bytes=48 * 1024 * 1024
        ),
        cost_estimate=pl.CostEstimate(flops=2_500_000_000, bytes_accessed=3_000_000, transcendentals=200_000),
    )(queries, passages, pool, positives.reshape(1, Q), weights.reshape(1, Q), requests)


def solution(mesh):
    rows = P(("group", "member"), None)
    flat = P(("group", "member"))
    return jax.shard_map(
        per_device,
        mesh=mesh,
        in_specs=(rows, rows, rows, flat, flat, rows),
        out_specs=(rows, rows, rows),
        check_vma=False,
    )
```

```python
import jax
import jax.numpy as jnp
from jax import lax
from jax.experimental import pallas as pl
from jax.experimental.pallas import tpu as pltpu
from jax.sharding import PartitionSpec as P

MESH = pl.DeviceIdType.MESH
F32 = jnp.float32
BF16 = jnp.bfloat16

D = 4096
Q = 48
HB = 128
W = 1024
HW = 512
HALF = D // 2
N = 8
HOPS = N // 2
FACTOR = D ** (-0.5)
NEG = -1e30
VMEM_LIMIT = 40 * 1024 * 1024


def nt(a, b):
    return lax.dot_general(a, b, (((1,), (1,)), ((), ())), preferred_element_type=F32)


def nn(a, b):
    return lax.dot_general(a, b, (((1,), (0,)), ((), ())), preferred_element_type=F32)


def tn(a, b):
    return lax.dot_general(a, b, (((0,), (0,)), ((), ())), preferred_element_type=F32)


def slot_of(rel):
    rel = rel % N
    return 0 if rel == 0 else (2 * rel - 1 if rel <= HOPS else 2 * (N - rel))


def rel_of(slot):
    return (slot + 1) // 2 if slot % 2 else (N - slot // 2) % N


SUM_PIECES = (6, 4, 2, 0)


def loop(n, body):
    lax.fori_loop(0, n, lambda i, _: (body(i), 0)[1], 0)


def cols(i, size):
    return pl.ds(pl.multiple_of(i * size, size), size)


def kernel(
    q_ref, p_ref, pool_ref, pos_ref, w_ref, req_ref,
    gq_ref, gp_ref, gpool_ref,
    q_all, pool2, ga, gb, meta, sc, pb, part, rx, st_out, st, ls, p_in, pos_in, w_in, req_in,
    q4, tin, cin, gpa, gpb, ra, rb, sa, sb, sa_in, sb_in,
    gq_acc, cb, gpo_out, gpo_in, gpo_acc,
    loc, qs, qr, ps, pr, ms, mr, a1s, a1r, b1s, b1r, ags, agr, sts, str_, lss, lsr,
    pts, ptr, gps, gpr, rss, rsr, a2s, a2r, b2s, b2r,
):
    g = lax.axis_index("group")
    mem = lax.axis_index("member")
    x, c = lax.div(g, 2), lax.rem(g, 2)
    y, z = lax.div(mem, N), lax.rem(mem, N)
    right = (lax.rem(x + 1, 4) * 2 + c, mem)
    left = (lax.rem(x + 3, 4) * 2 + c, mem)
    opp = (lax.rem(x + 2, 4) * 2 + c, mem)
    mate_group = x * 2 + 1 - c
    mate = (mate_group, mem)

    def yd(d):
        return (g, lax.rem(y + d, N) * N + z)

    def zd(d):
        return (g, y * N + lax.rem(z + d, N))

    def rc(src, dst, ssem, rsem, dev):
        return pltpu.make_async_remote_copy(
            src_ref=src, dst_ref=dst, send_sem=ssem, recv_sem=rsem,
            device_id=dev, device_id_type=MESH,
        )

    sent = []

    def go(copy):
        copy.start()
        sent.append(copy)

    waited = set()

    def arrived(ref, sem, key=None):
        if key is not None:
            if key in waited:
                return
            waited.add(key)
        rc(ref, ref, sem, sem, right).wait_recv()

    load_p = pltpu.make_async_copy(p_ref, p_in, loc.at[5])
    load_p.start()
    load_req = pltpu.make_async_copy(req_ref, req_in, loc.at[2])
    load_pos = pltpu.make_async_copy(pos_ref, pos_in, loc.at[3])
    load_w = pltpu.make_async_copy(w_ref, w_in, loc.at[4])
    load_req.start()
    load_pos.start()
    load_w.start()
    barrier = pltpu.get_barrier_semaphore()
    for dev in (right, left, opp, mate):
        pl.semaphore_signal(barrier, inc=1, device_id=dev, device_id_type=MESH)
    for d in range(1, N):
        pl.semaphore_signal(barrier, inc=1, device_id=yd(d), device_id_type=MESH)
        pl.semaphore_signal(barrier, inc=1, device_id=zd(d), device_id_type=MESH)

    load_q = pltpu.make_async_copy(q_ref, q_all.at[0], loc.at[0])
    load_pool = pltpu.make_async_copy(pool_ref, pool2.at[pl.ds(0, HB)], loc.at[1])
    load_q.start()
    load_pool.start()

    load_p.wait()
    pf = p_in[...].astype(F32)
    row16 = lax.broadcasted_iota(jnp.int32, (16, HW), 0)

    def fold(off):
        acc = jnp.zeros((16, HW), F32)
        for r in range(4):
            for k in range(4):
                piece = pf[r:r + 1, k * W + off:k * W + off + HW]
                acc = jnp.where(row16 == 4 * r + k, piece, acc)
        return acc.astype(BF16)

    ga[0, 0] = fold(0)
    gb[0, 0] = fold(HW)
    meta[0] = jnp.zeros((8, 128), F32)
    load_req.wait()
    load_pos.wait()
    load_w.wait()
    meta[0, 0:1, 0:8] = req_in[...].astype(F32)

    pl.semaphore_wait(barrier, 4 + 2 * (N - 1))

    for d in (4, 3, 5, 2, 6, 1, 7):
        go(rc(ga.at[0, 0], ga.at[0, slot_of(d)], a1s.at[d], a1r.at[d], zd(d)))
        go(rc(gb.at[0, 0], gb.at[slot_of(d), 0], b1s.at[d], b1r.at[d], yd(d)))
    go(rc(q_ref, q_all.at[1], qs.at[0], qr.at[0], right))
    go(rc(q_ref, q_all.at[2], qs.at[1], qr.at[1], left))
    go(rc(meta.at[0], meta.at[1], ms.at[0], mr.at[0], right))
    go(rc(meta.at[0], meta.at[2], ms.at[1], mr.at[1], left))
    go(rc(meta.at[0], meta.at[3], ms.at[2], mr.at[2], opp))
    go(rc(pool_ref, pool2.at[pl.ds(HB, HB)], ps.at[0], pr.at[0], mate))
    go(rc(q_ref, q_all.at[3], qs.at[2], qr.at[2], opp))

    def ring_view(flow, rel, part):
        near = pl.ds(4 * part, 4)
        return ga.at[slot_of(rel), near] if flow < 2 else gb.at[near, slot_of(rel)]

    def ring_go(flow, src_rel, dst_rel, hops, step, part):
        hop = N - hops if flow % 2 else hops
        sem = 2 * step + part
        go(rc(
            ring_view(flow, src_rel, part), ring_view(flow, dst_rel, part),
            ags.at[flow, sem], agr.at[flow, sem], yd(hop) if flow < 2 else zd(hop),
        ))

    def ring_arrived(flow, step, part):
        rel = (step + 1) * (1 if flow % 2 == 0 else -1)
        arrived(ring_view(flow, rel, part), agr.at[flow, 2 * step + part], ("ring", flow, step, part))

    def ring_step(step, part):
        for flow in range(4):
            sign = 1 if flow % 2 == 0 else -1
            if step == 0:
                for slot in range(max(4 * part, 1), 4 * part + 4):
                    rel = rel_of(slot)
                    if flow < 2:
                        arrived(ga.at[0, slot], a1r.at[rel], ("a1", rel))
                    else:
                        arrived(gb.at[slot, 0], b1r.at[rel], ("b1", rel))
            else:
                ring_arrived(flow, step - 1, part)
            ring_go(flow, sign * step, sign * (step + 1), 1, step, part)
            if step == 2 and flow % 2 == part:
                ring_go(flow, sign * 2, 4, 2, 3, part)

    ring_step(0, 0)
    ring_step(0, 1)

    lane256 = lax.broadcasted_iota(jnp.int32, (1, 2 * HB), 1)
    lane128 = lax.broadcasted_iota(jnp.int32, (1, 128), 1)

    def hard(slot):
        def body(i, acc):
            at = cols(i, 1024)
            return acc + nt(q_all[slot, :, at], pool2[:, at])

        scores = lax.fori_loop(0, 4, body, jnp.zeros((Q, 2 * HB), F32)) * FACTOR
        line = meta[slot, 0:1, :]
        here = jnp.sum(jnp.where(lane128 == g, line, 0.0), axis=1, keepdims=True)
        there = jnp.sum(jnp.where(lane128 == mate_group, line, 0.0), axis=1, keepdims=True)
        asked = jnp.where(lane256 < HB, here, there) != 0.0
        scores = jnp.where(asked, scores, NEG)
        sc[slot] = scores
        top = jnp.max(scores, axis=1, keepdims=True)
        probs = jnp.where(asked, jnp.exp(scores - top), 0.0)
        total = jnp.sum(probs, axis=1, keepdims=True)
        pb[slot] = probs.astype(BF16)
        st_out[slot] = jnp.where(lane128 < 64, top, total)

    def partial(slot, dest, theirs):
        for half in (0, 1):
            def body(i):
                at = cols(i + 4 * half, 512)
                part[slot, :, at] = nn(pb[slot], pool2[:, at]).astype(BF16)

            loop(4, body)
            at, sem = pl.ds(half * HALF, HALF), 2 * theirs + half
            go(rc(part.at[slot, :, at], rx.at[theirs, :, at], pts.at[sem], ptr.at[sem], dest))

    load_q.wait()
    load_pool.wait()
    arrived(pool2.at[pl.ds(HB, HB)], pr.at[0])
    hard(0)
    for k in range(4):
        q4[k * Q:(k + 1) * Q, :] = q_all[0, :, k * W:(k + 1) * W]
    ring_step(1, 0)
    ring_step(1, 1)

    arrived(q_all.at[1], qr.at[0])
    arrived(meta.at[1], mr.at[0])
    hard(1)
    go(rc(st_out.at[1], st.at[2], sts.at[0], str_.at[0], left))
    ring_step(2, 0)
    arrived(q_all.at[2], qr.at[1])
    arrived(meta.at[2], mr.at[1])
    hard(2)
    go(rc(st_out.at[2], st.at[1], sts.at[1], str_.at[1], right))
    ring_step(2, 1)

    arrived(q_all.at[3], qr.at[2])
    arrived(meta.at[3], mr.at[2])
    hard(3)
    go(rc(st_out.at[3], st.at[3], sts.at[2], str_.at[2], opp))
    partial(1, left, 1)
    partial(2, right, 0)

    for flow in range(4):
        for half in (0, 1):
            ring_arrived(flow, 2, half)
        ring_arrived(flow, 3, flow % 2)
    mod4 = lax.rem(lane256, 4)

    def in_block(b):
        pa = ga[pl.ds(2 * b, 2)].reshape(256, HW)
        pbk = gb[pl.ds(2 * b, 2)].reshape(256, HW)
        s = nt(q4[:, 0:HW], pa) + nt(q4[:, HW:W], pbk)
        t = jnp.where(mod4 == 0, s[0:Q], 0.0)
        for k in range(1, 4):
            t = jnp.where(mod4 == k, s[k * Q:(k + 1) * Q], t)
        t = t + jnp.where(lax.rem(mod4, 2) == 0, pltpu.roll(t, 255, 1), pltpu.roll(t, 1, 1))
        t = t + jnp.where(mod4 < 2, pltpu.roll(t, 254, 1), pltpu.roll(t, 2, 1))
        tin[:, cols(b, 256)] = t * FACTOR

    loop(4, in_block)

    for i in range(3):
        arrived(st.at[(2, 1, 3)[i]], str_.at[i])
    tops = [st_out[0][:, 0:1]] + [st[i][:, 0:1] for i in (1, 2, 3)]
    sums = [st_out[0][:, 64:65]] + [st[i][:, 64:65] for i in (1, 2, 3)]
    t_in = tin[...]
    highest = jnp.max(t_in, axis=1, keepdims=True)
    for t in tops:
        highest = jnp.maximum(highest, t)
    lane1024 = lax.broadcasted_iota(jnp.int32, (1, W), 1)
    quarter = lax.rem(lane1024, 4)
    totals = jnp.sum(
        jnp.where(quarter == 0, jnp.exp(t_in - highest), 0.0), axis=1, keepdims=True
    )
    for t, s in zip(tops, sums):
        totals = totals + s * jnp.exp(t - highest)
    logsum = highest + jnp.log(totals)
    eye = lax.broadcasted_iota(jnp.int32, (Q, Q), 0) == lax.broadcasted_iota(jnp.int32, (Q, Q), 1)
    weight = jnp.sum(jnp.where(eye, w_in[...], 0.0), axis=1, keepdims=True)
    positive = jnp.sum(jnp.where(eye, pos_in[...], 0), axis=1, keepdims=True)
    ls[0] = jnp.where(lane128 < 64, logsum, weight)
    go(rc(ls.at[0], ls.at[1], lss.at[0], lsr.at[0], right))
    go(rc(ls.at[0], ls.at[2], lss.at[1], lsr.at[1], left))
    go(rc(ls.at[0], ls.at[3], lss.at[2], lsr.at[2], opp))

    def rel_at(slot):
        half = lax.div(slot + 1, 2)
        return jnp.where(lax.rem(slot, 2) == 1, half, lax.rem(N - half, N))

    from_y = lax.rem(y + N - rel_at(lax.div(lane1024, 128)), N)
    from_z = lax.rem(z + N - rel_at(lax.rem(lax.div(lane1024, 16), N)), N)
    passage = (from_y * N + from_z) * 4 + lax.rem(lax.div(lane1024, 4), 4)
    one_hot = (passage == positive).astype(F32)
    coefs = weight * (jnp.exp(t_in - logsum) - one_hot) * FACTOR
    for k in range(4):
        cin[k * Q:(k + 1) * Q, :] = jnp.where(quarter == k, coefs, 0.0).astype(BF16)

    def gp_block(b):
        rows = tn(cin[:, cols(b, 128)], q4[...]).astype(BF16)
        gpa[b] = rows[:, 0:HW].reshape(N, 16, HW)
        gpb[b] = rows[:, HW:W].reshape(N, 16, HW)

    def sum_view(flow, d, u):
        slot = slot_of(N - d if flow % 2 == 0 else d)
        pair = pl.ds(SUM_PIECES[u], 2)
        return gpa.at[pair, slot] if flow < 2 else gpb.at[slot, pair]

    def sum_slot(flow, kind, u):
        return (ra if flow < 2 else rb).at[flow % 2, kind, pl.ds(SUM_PIECES[u], 2)]

    def sum_go(flow, d, kind, hops, u):
        hop = hops if flow % 2 == 0 else N - hops
        sem = kind * 4 + u
        go(rc(
            sum_view(flow, d, u), sum_slot(flow, kind, u), rss.at[flow, sem], rsr.at[flow, sem],
            zd(hop) if flow < 2 else yd(hop),
        ))

    def sum_add(flow, d, kind, u):
        arrived(sum_slot(flow, kind, u), rsr.at[flow, kind * 4 + u])
        view = sum_view(flow, d, u)
        view[...] = view[...] + sum_slot(flow, kind, u)[...]

    def from_four(flow, u):
        return (u < 2) == (flow % 2 == 0)

    def sum_first(flows):
        for u in range(4):
            for flow in flows:
                if from_four(flow, u):
                    sum_go(flow, 4, 1, 2, u)
                sum_go(flow, 3, 0, 1, u)

    def sum_second():
        for u in range(4):
            for flow in range(4):
                sum_add(flow, 2, 0, u)
                if from_four(flow, u):
                    sum_add(flow, 2, 1, u)
                sum_go(flow, 2, 2, 1, u)

    def sum_third():
        for u in range(4):
            for flow in range(4):
                sum_add(flow, 1, 2, u)
                sum_go(flow, 1, 3, 1, u)

    loop(3, lambda i: gp_block(N - 1 - i))
    sum_first((2, 3))
    loop(N - 3, gp_block)
    sum_first((0, 1))

    partial(3, opp, 2)

    def coef_rows(slot):
        lsum, wt = ls[slot][:, 0:1], ls[slot][:, 64:65]
        cb[slot * Q:(slot + 1) * Q, :] = (wt * jnp.exp(sc[slot] - lsum) * FACTOR).astype(BF16)

    coef_rows(0)

    def own_rows(i):
        at = cols(i, 512)
        gq_acc[:, at] = nn(cb[0:Q, :], pool2[:, at])

    loop(8, own_rows)

    sum_second()

    for h, ref in ((0, ga), (1, gb)):
        for n in range(2):
            rows = nn(cin[...], ref[:, :, :, n * 256:(n + 1) * 256].reshape(W, 256))
            for k in range(4):
                to = pl.ds(k * W + h * HW + n * 256, 256)
                gq_acc[:, to] = gq_acc[:, to] + rows[k * Q:(k + 1) * Q]

    sum_third()

    for i in range(3):
        arrived(ls.at[i + 1], lsr.at[i])
        coef_rows(i + 1)

    def far_pool(i):
        at = cols(i, 512)
        gpo_out[:, at] = tn(cb[:, HB:2 * HB], q_all[:, :, at].reshape(4 * Q, 512)).astype(BF16)

    loop(8, far_pool)
    go(rc(gpo_out, gpo_in, gps.at[0], gpr.at[0], mate))

    def near_pool(i):
        at = cols(i, 512)
        gpo_acc[:, at] = tn(cb[:, 0:HB], q_all[:, :, at].reshape(4 * Q, 512))

    for u in range(4):
        for flow in range(4):
            arrived(sum_slot(flow, 3, u), rsr.at[flow, 12 + u])
        first = SUM_PIECES[u]
        pair = pl.ds(first, 2)
        sa[pair] = (
            gpa[pair, 0].astype(F32) + ra[0, 3, pair].astype(F32)
            + ra[1, 3, pair].astype(F32)
        ).astype(BF16)
        sb[pair] = (
            gpb[0, pair].astype(F32) + rb[0, 3, pair].astype(F32)
            + rb[1, 3, pair].astype(F32)
        ).astype(BF16)
        for slot in (first + 1, first):
            if slot > 0:
                d = N - rel_of(slot)
                go(rc(sa.at[slot], sa_in.at[slot], a2s.at[slot], a2r.at[slot], yd(d)))
                go(rc(sb.at[slot], sb_in.at[slot], b2s.at[slot], b2r.at[slot], zd(d)))

    loop(8, near_pool)
    arrived(gpo_in, gpr.at[0])

    def pool_sum(i):
        at = cols(i, 512)
        gpool_ref[:, at] = (gpo_acc[:, at] + gpo_in[:, at].astype(F32)).astype(BF16)

    loop(8, pool_sum)

    scales = [weight * FACTOR * jnp.exp(t - logsum) for t in tops[1:]]
    for half in (0, 1):
        for way in range(3):
            arrived(rx.at[way, :, pl.ds(half * HALF, HALF)], ptr.at[2 * way + half])

    def finish(i):
        at = cols(i, 512)
        acc = gq_acc[:, at]
        for way in range(3):
            acc = acc + rx[way, :, at].astype(F32) * scales[way]
        gq_ref[:, at] = acc.astype(BF16)

    loop(8, finish)

    row4 = lax.broadcasted_iota(jnp.int32, (4, HW), 0)
    for h, own, held, sem in ((0, sa[0], sa_in, a2r), (1, sb[0], sb_in, b2r)):
        acc = own.astype(F32)
        for slot in range(1, N):
            arrived(held.at[slot], sem.at[slot])
            acc = acc + held[slot].astype(F32)
        for k in range(4):
            out = jnp.zeros((4, HW), F32)
            for r in range(4):
                out = jnp.where(row4 == r, acc[4 * r + k:4 * r + k + 1, :], out)
            gp_ref[:, k * W + h * HW:k * W + (h + 1) * HW] = out.astype(BF16)

    for copy in sent:
        copy.wait_send()


def store(q_in, p_in, pool_in, q_out, p_out, pool_out, sem):
    pairs = ((pool_in, pool_out), (q_in, q_out), (p_in, p_out))
    copies = [pltpu.make_async_copy(src, dst, sem.at[i]) for i, (src, dst) in enumerate(pairs)]
    for copy in copies:
        copy.start()
    for copy in copies:
        copy.wait()


def per_device(queries, passages, pool, positives, weights, requests):
    dma = pltpu.SemaphoreType.DMA
    v = pltpu.VMEM
    scratch = [
        v((4, Q, D), BF16),
        v((2 * HB, D), BF16),
        v((N, N, 16, HW), BF16),
        v((N, N, 16, HW), BF16),
        v((4, 8, 128), F32),
        v((4, Q, 2 * HB), F32),
        v((4, Q, 2 * HB), BF16),
        v((4, Q, D), BF16),
        v((3, Q, D), BF16),
        v((4, Q, 128), F32),
        v((4, Q, 128), F32),
        v((4, Q, 128), F32),
        v((4, D), BF16),
        v((1, Q), jnp.int32),
        v((1, Q), F32),
        v((1, 8), jnp.int32),
        v((4 * Q, W), BF16),
        v((Q, W), F32),
        v((4 * Q, W), BF16),
        v((N, N, 16, HW), BF16),
        v((N, N, 16, HW), BF16),
        v((2, 4, N, 16, HW), BF16),
        v((2, 4, N, 16, HW), BF16),
        v((N, 16, HW), BF16),
        v((N, 16, HW), BF16),
        v((N, 16, HW), BF16),
        v((N, 16, HW), BF16),
        v((Q, D), F32),
        v((4 * Q, 2 * HB), BF16),
        v((HB, D), BF16),
        v((HB, D), BF16),
        v((HB, D), F32),
        dma((6,)),
        dma((3,)), dma((3,)),
        dma((1,)), dma((1,)),
        dma((3,)), dma((3,)),
        dma((N,)), dma((N,)), dma((N,)), dma((N,)),
        dma((4, 8)), dma((4, 8)),
        dma((3,)), dma((3,)),
        dma((3,)), dma((3,)),
        dma((6,)), dma((6,)),
        dma((1,)), dma((1,)),
        dma((4, 16)), dma((4, 16)),
        dma((N,)), dma((N,)), dma((N,)), dma((N,)),
    ]
    hbm = pl.BlockSpec(memory_space=pltpu.HBM)
    vmem = pl.BlockSpec(memory_space=pltpu.VMEM)
    outs = pl.pallas_call(
        kernel,
        out_shape=(
            jax.ShapeDtypeStruct((Q, D), BF16),
            jax.ShapeDtypeStruct((4, D), BF16),
            jax.ShapeDtypeStruct((HB, D), BF16),
        ),
        in_specs=[hbm] * 6,
        out_specs=(vmem,) * 3,
        scratch_shapes=scratch,
        compiler_params=pltpu.CompilerParams(
            collective_id=0, has_side_effects=True, vmem_limit_bytes=VMEM_LIMIT
        ),
        cost_estimate=pl.CostEstimate(flops=2_500_000_000, bytes_accessed=3_000_000, transcendentals=200_000),
    )(*(
        pltpu.with_memory_space_constraint(a, pltpu.HBM)
        for a in (queries, passages, pool, positives.reshape(1, Q), weights.reshape(1, Q), requests)
    ))
    return pl.pallas_call(
        store,
        out_shape=tuple(jax.ShapeDtypeStruct(o.shape, o.dtype) for o in outs),
        in_specs=[vmem] * 3,
        out_specs=(pl.BlockSpec(memory_space=pl.ANY),) * 3,
        scratch_shapes=[dma((3,))],
        compiler_params=pltpu.CompilerParams(vmem_limit_bytes=1024 * 1024),
    )(*outs)


def solution(mesh):
    rows = P(("group", "member"), None)
    flat = P(("group", "member"))
    return jax.shard_map(
        per_device,
        mesh=mesh,
        in_specs=(rows, rows, rows, flat, flat, rows),
        out_specs=(rows, rows, rows),
        check_vma=False,
    )
```

```python
import jax
import jax.numpy as jnp
from jax import lax
from jax.experimental import pallas as pl
from jax.experimental.pallas import tpu as pltpu
from jax.sharding import PartitionSpec as P

MESH = pl.DeviceIdType.MESH
F32 = jnp.float32
BF16 = jnp.bfloat16

D = 4096
Q = 48
HB = 128
W = 1024
HW = 512
HALF = D // 2
N = 8
HOPS = N // 2
FACTOR = D ** (-0.5)
NEG = -1e30
VMEM_LIMIT = 40 * 1024 * 1024


def nt(a, b):
    return lax.dot_general(a, b, (((1,), (1,)), ((), ())), preferred_element_type=F32)


def nn(a, b):
    return lax.dot_general(a, b, (((1,), (0,)), ((), ())), preferred_element_type=F32)


def tn(a, b):
    return lax.dot_general(a, b, (((0,), (0,)), ((), ())), preferred_element_type=F32)


def slot_of(rel):
    rel = rel % N
    return 0 if rel == 0 else (2 * rel - 1 if rel <= HOPS else 2 * (N - rel))


def rel_of(slot):
    return (slot + 1) // 2 if slot % 2 else (N - slot // 2) % N


SUM_PIECES = (6, 4, 2, 0)


def loop(n, body):
    for i in range(n):
        body(i)


def cols(i, size):
    return pl.ds(i * size, size)


def kernel(
    q_ref, p_ref, pool_ref, pos_ref, w_ref, req_ref,
    gq_ref, gp_ref, gpool_ref,
    q_all, pool2, ga, gb, meta, sc, pb, part, rx, st_out, st, ls, p_in, pos_in, w_in, req_in,
    q4, tin, cin, gpa, gpb, ra, rb, sa, sb, sa_in, sb_in,
    gq_acc, cb, gpo_out, gpo_in, gpo_acc,
    loc, qs, qr, ps, pr, ms, mr, a1s, a1r, b1s, b1r, ags, agr, sts, str_, lss, lsr,
    pts, ptr, gps, gpr, rss, rsr, a2s, a2r, b2s, b2r,
):
    g = lax.axis_index("group")
    mem = lax.axis_index("member")
    x, c = lax.div(g, 2), lax.rem(g, 2)
    y, z = lax.div(mem, N), lax.rem(mem, N)
    right = (lax.rem(x + 1, 4) * 2 + c, mem)
    left = (lax.rem(x + 3, 4) * 2 + c, mem)
    opp = (lax.rem(x + 2, 4) * 2 + c, mem)
    mate_group = x * 2 + 1 - c
    mate = (mate_group, mem)

    def yd(d):
        return (g, lax.rem(y + d, N) * N + z)

    def zd(d):
        return (g, y * N + lax.rem(z + d, N))

    def rc(src, dst, ssem, rsem, dev):
        return pltpu.make_async_remote_copy(
            src_ref=src, dst_ref=dst, send_sem=ssem, recv_sem=rsem,
            device_id=dev, device_id_type=MESH,
        )

    sent = []

    def go(copy):
        copy.start()
        sent.append(copy)

    waited = set()

    def arrived(ref, sem, key=None):
        if key is not None:
            if key in waited:
                return
            waited.add(key)
        rc(ref, ref, sem, sem, right).wait_recv()

    def all_sent(copies):
        for copy in copies:
            copy.wait_send()

    load_p = pltpu.make_async_copy(p_ref, p_in, loc.at[5])
    load_p.start()
    load_req = pltpu.make_async_copy(req_ref, req_in, loc.at[2])
    load_pos = pltpu.make_async_copy(pos_ref, pos_in, loc.at[3])
    load_w = pltpu.make_async_copy(w_ref, w_in, loc.at[4])
    load_req.start()
    load_pos.start()
    load_w.start()
    barrier = pltpu.get_barrier_semaphore()
    for dev in (right, left, opp, mate):
        pl.semaphore_signal(barrier, inc=1, device_id=dev, device_id_type=MESH)
    for d in range(1, N):
        pl.semaphore_signal(barrier, inc=1, device_id=yd(d), device_id_type=MESH)
        pl.semaphore_signal(barrier, inc=1, device_id=zd(d), device_id_type=MESH)

    load_q = pltpu.make_async_copy(q_ref, q_all.at[0], loc.at[0])
    load_pool = pltpu.make_async_copy(pool_ref, pool2.at[pl.ds(0, HB)], loc.at[1])
    load_q.start()
    load_pool.start()

    load_p.wait()
    pf = p_in[...].astype(F32)
    row16 = lax.broadcasted_iota(jnp.int32, (16, HW), 0)

    def fold(off):
        acc = jnp.zeros((16, HW), F32)
        for r in range(4):
            for k in range(4):
                piece = pf[r:r + 1, k * W + off:k * W + off + HW]
                acc = jnp.where(row16 == 4 * r + k, piece, acc)
        return acc.astype(BF16)

    ga[0, 0] = fold(0)
    gb[0, 0] = fold(HW)
    meta[0] = jnp.zeros((8, 128), F32)
    load_req.wait()
    load_pos.wait()
    load_w.wait()
    meta[0, 0:1, 0:8] = req_in[...].astype(F32)

    pl.semaphore_wait(barrier, 4 + 2 * (N - 1))

    for d in (4, 3, 5, 2, 6, 1, 7):
        go(rc(ga.at[0, 0], ga.at[0, slot_of(d)], a1s.at[d], a1r.at[d], zd(d)))
        go(rc(gb.at[0, 0], gb.at[slot_of(d), 0], b1s.at[d], b1r.at[d], yd(d)))
    go(rc(q_ref, q_all.at[1], qs.at[0], qr.at[0], right))
    go(rc(q_ref, q_all.at[2], qs.at[1], qr.at[1], left))
    go(rc(meta.at[0], meta.at[1], ms.at[0], mr.at[0], right))
    go(rc(meta.at[0], meta.at[2], ms.at[1], mr.at[1], left))
    go(rc(meta.at[0], meta.at[3], ms.at[2], mr.at[2], opp))
    go(rc(pool_ref, pool2.at[pl.ds(HB, HB)], ps.at[0], pr.at[0], mate))
    go(rc(q_ref, q_all.at[3], qs.at[2], qr.at[2], opp))

    def ring_view(flow, rel, part):
        near = pl.ds(4 * part, 4)
        return ga.at[slot_of(rel), near] if flow < 2 else gb.at[near, slot_of(rel)]

    def ring_go(flow, src_rel, dst_rel, hops, step, part):
        hop = N - hops if flow % 2 else hops
        sem = 2 * step + part
        go(rc(
            ring_view(flow, src_rel, part), ring_view(flow, dst_rel, part),
            ags.at[flow, sem], agr.at[flow, sem], yd(hop) if flow < 2 else zd(hop),
        ))

    def ring_arrived(flow, step, part):
        rel = (step + 1) * (1 if flow % 2 == 0 else -1)
        arrived(ring_view(flow, rel, part), agr.at[flow, 2 * step + part], ("ring", flow, step, part))

    def ring_step(step, part):
        for flow in range(4):
            sign = 1 if flow % 2 == 0 else -1
            if step == 0:
                for slot in range(max(4 * part, 1), 4 * part + 4):
                    rel = rel_of(slot)
                    if flow < 2:
                        arrived(ga.at[0, slot], a1r.at[rel], ("a1", rel))
                    else:
                        arrived(gb.at[slot, 0], b1r.at[rel], ("b1", rel))
            else:
                ring_arrived(flow, step - 1, part)
            ring_go(flow, sign * step, sign * (step + 1), 1, step, part)
            if step == 2 and flow % 2 == part:
                ring_go(flow, sign * 2, 4, 2, 3, part)

    ring_step(0, 0)
    ring_step(0, 1)

    lane256 = lax.broadcasted_iota(jnp.int32, (1, 2 * HB), 1)
    lane128 = lax.broadcasted_iota(jnp.int32, (1, 128), 1)

    def hard(slot):
        scores = nt(q_all[slot], pool2[...]) * FACTOR
        line = meta[slot, 0:1, :]
        here = jnp.sum(jnp.where(lane128 == g, line, 0.0), axis=1, keepdims=True)
        there = jnp.sum(jnp.where(lane128 == mate_group, line, 0.0), axis=1, keepdims=True)
        asked = jnp.where(lane256 < HB, here, there) != 0.0
        scores = jnp.where(asked, scores, NEG)
        sc[slot] = scores
        top = jnp.max(scores, axis=1, keepdims=True)
        probs = jnp.where(asked, jnp.exp(scores - top), 0.0)
        total = jnp.sum(probs, axis=1, keepdims=True)
        pb[slot] = probs.astype(BF16)
        st_out[slot] = jnp.where(lane128 < 64, top, total)

    def partial(slot, dest, theirs):
        for half in (0, 1):
            def body(i):
                at = cols(i + 4 * half, 512)
                part[slot, :, at] = nn(pb[slot], pool2[:, at]).astype(BF16)

            loop(4, body)
            at, sem = pl.ds(half * HALF, HALF), 2 * theirs + half
            go(rc(part.at[slot, :, at], rx.at[theirs, :, at], pts.at[sem], ptr.at[sem], dest))

    load_q.wait()
    load_pool.wait()
    arrived(pool2.at[pl.ds(HB, HB)], pr.at[0])
    hard(0)
    for k in range(4):
        q4[k * Q:(k + 1) * Q, :] = q_all[0, :, k * W:(k + 1) * W]
    for step in (1, 2):
        ring_step(step, 0)
        ring_step(step, 1)

    arrived(q_all.at[1], qr.at[0])
    arrived(meta.at[1], mr.at[0])
    hard(1)
    go(rc(st_out.at[1], st.at[2], sts.at[0], str_.at[0], left))
    arrived(q_all.at[2], qr.at[1])
    arrived(meta.at[2], mr.at[1])
    hard(2)
    go(rc(st_out.at[2], st.at[1], sts.at[1], str_.at[1], right))

    arrived(q_all.at[3], qr.at[2])
    arrived(meta.at[3], mr.at[2])
    hard(3)
    go(rc(st_out.at[3], st.at[3], sts.at[2], str_.at[2], opp))
    early = list(sent)
    sent.clear()

    for flow in range(4):
        for half in (0, 1):
            ring_arrived(flow, 2, half)
        ring_arrived(flow, 3, flow % 2)
    mod4 = lax.rem(lane256, 4)

    def in_block(b):
        pa = ga[pl.ds(2 * b, 2)].reshape(256, HW)
        pbk = gb[pl.ds(2 * b, 2)].reshape(256, HW)
        s = nt(q4[:, 0:HW], pa) + nt(q4[:, HW:W], pbk)
        t = jnp.where(mod4 == 0, s[0:Q], 0.0)
        for k in range(1, 4):
            t = jnp.where(mod4 == k, s[k * Q:(k + 1) * Q], t)
        t = t + jnp.where(lax.rem(mod4, 2) == 0, pltpu.roll(t, 255, 1), pltpu.roll(t, 1, 1))
        t = t + jnp.where(mod4 < 2, pltpu.roll(t, 254, 1), pltpu.roll(t, 2, 1))
        tin[:, cols(b, 256)] = t * FACTOR

    loop(4, in_block)

    for i in range(3):
        arrived(st.at[(2, 1, 3)[i]], str_.at[i])
    tops = [st_out[0][:, 0:1]] + [st[i][:, 0:1] for i in (1, 2, 3)]
    sums = [st_out[0][:, 64:65]] + [st[i][:, 64:65] for i in (1, 2, 3)]
    t_in = tin[...]
    highest = jnp.max(t_in, axis=1, keepdims=True)
    for t in tops:
        highest = jnp.maximum(highest, t)
    lane1024 = lax.broadcasted_iota(jnp.int32, (1, W), 1)
    quarter = lax.rem(lane1024, 4)
    totals = jnp.sum(
        jnp.where(quarter == 0, jnp.exp(t_in - highest), 0.0), axis=1, keepdims=True
    )
    for t, s in zip(tops, sums):
        totals = totals + s * jnp.exp(t - highest)
    logsum = highest + jnp.log(totals)
    eye = lax.broadcasted_iota(jnp.int32, (Q, Q), 0) == lax.broadcasted_iota(jnp.int32, (Q, Q), 1)
    weight = jnp.sum(jnp.where(eye, w_in[...], 0.0), axis=1, keepdims=True)
    positive = jnp.sum(jnp.where(eye, pos_in[...], 0), axis=1, keepdims=True)
    ls[0] = jnp.where(lane128 < 64, logsum, weight)
    go(rc(ls.at[0], ls.at[1], lss.at[0], lsr.at[0], right))
    go(rc(ls.at[0], ls.at[2], lss.at[1], lsr.at[1], left))
    go(rc(ls.at[0], ls.at[3], lss.at[2], lsr.at[2], opp))

    def rel_at(slot):
        half = lax.div(slot + 1, 2)
        return jnp.where(lax.rem(slot, 2) == 1, half, lax.rem(N - half, N))

    from_y = lax.rem(y + N - rel_at(lax.div(lane1024, 128)), N)
    from_z = lax.rem(z + N - rel_at(lax.rem(lax.div(lane1024, 16), N)), N)
    passage = (from_y * N + from_z) * 4 + lax.rem(lax.div(lane1024, 4), 4)
    one_hot = (passage == positive).astype(F32)
    coefs = weight * (jnp.exp(t_in - logsum) - one_hot) * FACTOR
    for k in range(4):
        cin[k * Q:(k + 1) * Q, :] = jnp.where(quarter == k, coefs, 0.0).astype(BF16)

    def gp_block(b):
        rows = tn(cin[:, cols(b, 128)], q4[...]).astype(BF16)
        gpa[b] = rows[:, 0:HW].reshape(N, 16, HW)
        gpb[b] = rows[:, HW:W].reshape(N, 16, HW)

    def sum_view(flow, d, u):
        slot = slot_of(N - d if flow % 2 == 0 else d)
        pair = pl.ds(SUM_PIECES[u], 2)
        return gpa.at[pair, slot] if flow < 2 else gpb.at[slot, pair]

    def sum_slot(flow, kind, u):
        return (ra if flow < 2 else rb).at[flow % 2, kind, pl.ds(SUM_PIECES[u], 2)]

    def sum_go(flow, d, kind, hops, u):
        hop = hops if flow % 2 == 0 else N - hops
        sem = kind * 4 + u
        go(rc(
            sum_view(flow, d, u), sum_slot(flow, kind, u), rss.at[flow, sem], rsr.at[flow, sem],
            zd(hop) if flow < 2 else yd(hop),
        ))

    def sum_add(flow, d, kind, u):
        arrived(sum_slot(flow, kind, u), rsr.at[flow, kind * 4 + u])
        view = sum_view(flow, d, u)
        view[...] = view[...] + sum_slot(flow, kind, u)[...]

    def from_four(flow, u):
        return (u < 2) == (flow % 2 == 0)

    def sum_first(flows):
        for u in range(4):
            for flow in flows:
                if from_four(flow, u):
                    sum_go(flow, 4, 1, 2, u)
                sum_go(flow, 3, 0, 1, u)

    def sum_second():
        for u in range(4):
            for flow in range(4):
                sum_add(flow, 2, 0, u)
                if from_four(flow, u):
                    sum_add(flow, 2, 1, u)
                sum_go(flow, 2, 2, 1, u)

    def sum_third():
        for u in range(4):
            for flow in range(4):
                sum_add(flow, 1, 2, u)
                sum_go(flow, 1, 3, 1, u)

    loop(3, lambda i: gp_block(N - 1 - i))
    sum_first((2, 3))
    loop(N - 3, gp_block)
    sum_first((0, 1))

    partial(1, left, 1)
    partial(2, right, 0)
    partial(3, opp, 2)

    def coef_rows(slot):
        lsum, wt = ls[slot][:, 0:1], ls[slot][:, 64:65]
        cb[slot * Q:(slot + 1) * Q, :] = (wt * jnp.exp(sc[slot] - lsum) * FACTOR).astype(BF16)

    coef_rows(0)

    def own_rows(i):
        at = cols(i, 512)
        gq_acc[:, at] = nn(cb[0:Q, :], pool2[:, at])

    loop(8, own_rows)

    sum_second()

    for h, ref in ((0, ga), (1, gb)):
        for n in range(2):
            rows = nn(cin[...], ref[:, :, :, n * 256:(n + 1) * 256].reshape(W, 256))
            for k in range(4):
                to = pl.ds(k * W + h * HW + n * 256, 256)
                gq_acc[:, to] = gq_acc[:, to] + rows[k * Q:(k + 1) * Q]

    later = list(sent)
    sent.clear()
    sum_third()
    all_sent(early)

    for i in range(3):
        arrived(ls.at[i + 1], lsr.at[i])
        coef_rows(i + 1)

    def far_pool(i):
        at = cols(i, 512)
        gpo_out[:, at] = tn(cb[:, HB:2 * HB], q_all[:, :, at].reshape(4 * Q, 512)).astype(BF16)

    loop(8, far_pool)
    go(rc(gpo_out, gpo_in, gps.at[0], gpr.at[0], mate))

    def near_pool(i):
        at = cols(i, 512)
        gpo_acc[:, at] = tn(cb[:, 0:HB], q_all[:, :, at].reshape(4 * Q, 512))

    for u in range(4):
        for flow in range(4):
            arrived(sum_slot(flow, 3, u), rsr.at[flow, 12 + u])
        first = SUM_PIECES[u]
        pair = pl.ds(first, 2)
        sa[pair] = (
            gpa[pair, 0].astype(F32) + ra[0, 3, pair].astype(F32)
            + ra[1, 3, pair].astype(F32)
        ).astype(BF16)
        sb[pair] = (
            gpb[0, pair].astype(F32) + rb[0, 3, pair].astype(F32)
            + rb[1, 3, pair].astype(F32)
        ).astype(BF16)
        for slot in (first + 1, first):
            if slot > 0:
                d = N - rel_of(slot)
                go(rc(sa.at[slot], sa_in.at[slot], a2s.at[slot], a2r.at[slot], yd(d)))
                go(rc(sb.at[slot], sb_in.at[slot], b2s.at[slot], b2r.at[slot], zd(d)))

    loop(8, near_pool)
    all_sent(later)
    arrived(gpo_in, gpr.at[0])

    def pool_sum(i):
        at = cols(i, 512)
        gpool_ref[:, at] = (gpo_acc[:, at] + gpo_in[:, at].astype(F32)).astype(BF16)

    loop(8, pool_sum)

    scales = [weight * FACTOR * jnp.exp(t - logsum) for t in tops[1:]]
    for half in (0, 1):
        for way in range(3):
            arrived(rx.at[way, :, pl.ds(half * HALF, HALF)], ptr.at[2 * way + half])

    def finish(i):
        at = cols(i, 512)
        acc = gq_acc[:, at]
        for way in range(3):
            acc = acc + rx[way, :, at].astype(F32) * scales[way]
        gq_ref[:, at] = acc.astype(BF16)

    loop(8, finish)

    row4 = lax.broadcasted_iota(jnp.int32, (4, HW), 0)
    for h, own, held, sem in ((0, sa[0], sa_in, a2r), (1, sb[0], sb_in, b2r)):
        acc = own.astype(F32)
        for slot in range(1, N):
            arrived(held.at[slot], sem.at[slot])
            acc = acc + held[slot].astype(F32)
        for k in range(4):
            out = jnp.zeros((4, HW), F32)
            for r in range(4):
                out = jnp.where(row4 == r, acc[4 * r + k:4 * r + k + 1, :], out)
            gp_ref[:, k * W + h * HW:k * W + (h + 1) * HW] = out.astype(BF16)

    all_sent(sent)


def store(q_in, p_in, pool_in, q_out, p_out, pool_out, sem):
    pairs = ((pool_in, pool_out), (q_in, q_out), (p_in, p_out))
    copies = [pltpu.make_async_copy(src, dst, sem.at[i]) for i, (src, dst) in enumerate(pairs)]
    for copy in copies:
        copy.start()
    for copy in copies:
        copy.wait()


def per_device(queries, passages, pool, positives, weights, requests):
    dma = pltpu.SemaphoreType.DMA
    v = pltpu.VMEM
    scratch = [
        v((4, Q, D), BF16),
        v((2 * HB, D), BF16),
        v((N, N, 16, HW), BF16),
        v((N, N, 16, HW), BF16),
        v((4, 8, 128), F32),
        v((4, Q, 2 * HB), F32),
        v((4, Q, 2 * HB), BF16),
        v((4, Q, D), BF16),
        v((3, Q, D), BF16),
        v((4, Q, 128), F32),
        v((4, Q, 128), F32),
        v((4, Q, 128), F32),
        v((4, D), BF16),
        v((1, Q), jnp.int32),
        v((1, Q), F32),
        v((1, 8), jnp.int32),
        v((4 * Q, W), BF16),
        v((Q, W), F32),
        v((4 * Q, W), BF16),
        v((N, N, 16, HW), BF16),
        v((N, N, 16, HW), BF16),
        v((2, 4, N, 16, HW), BF16),
        v((2, 4, N, 16, HW), BF16),
        v((N, 16, HW), BF16),
        v((N, 16, HW), BF16),
        v((N, 16, HW), BF16),
        v((N, 16, HW), BF16),
        v((Q, D), F32),
        v((4 * Q, 2 * HB), BF16),
        v((HB, D), BF16),
        v((HB, D), BF16),
        v((HB, D), F32),
        dma((6,)),
        dma((3,)), dma((3,)),
        dma((1,)), dma((1,)),
        dma((3,)), dma((3,)),
        dma((N,)), dma((N,)), dma((N,)), dma((N,)),
        dma((4, 8)), dma((4, 8)),
        dma((3,)), dma((3,)),
        dma((3,)), dma((3,)),
        dma((6,)), dma((6,)),
        dma((1,)), dma((1,)),
        dma((4, 16)), dma((4, 16)),
        dma((N,)), dma((N,)), dma((N,)), dma((N,)),
    ]
    hbm = pl.BlockSpec(memory_space=pltpu.HBM)
    vmem = pl.BlockSpec(memory_space=pltpu.VMEM)
    outs = pl.pallas_call(
        kernel,
        out_shape=(
            jax.ShapeDtypeStruct((Q, D), BF16),
            jax.ShapeDtypeStruct((4, D), BF16),
            jax.ShapeDtypeStruct((HB, D), BF16),
        ),
        in_specs=[hbm] * 6,
        out_specs=(vmem,) * 3,
        scratch_shapes=scratch,
        compiler_params=pltpu.CompilerParams(
            collective_id=0, has_side_effects=True, vmem_limit_bytes=VMEM_LIMIT
        ),
        cost_estimate=pl.CostEstimate(flops=2_500_000_000, bytes_accessed=3_000_000, transcendentals=200_000),
    )(*(
        pltpu.with_memory_space_constraint(a, pltpu.HBM)
        for a in (queries, passages, pool, positives.reshape(1, Q), weights.reshape(1, Q), requests)
    ))
    return pl.pallas_call(
        store,
        out_shape=tuple(jax.ShapeDtypeStruct(o.shape, o.dtype) for o in outs),
        in_specs=[vmem] * 3,
        out_specs=(pl.BlockSpec(memory_space=pl.ANY),) * 3,
        scratch_shapes=[dma((3,))],
        compiler_params=pltpu.CompilerParams(vmem_limit_bytes=1024 * 1024),
    )(*outs)


def solution(mesh):
    rows = P(("group", "member"), None)
    flat = P(("group", "member"))
    return jax.shard_map(
        per_device,
        mesh=mesh,
        in_specs=(rows, rows, rows, flat, flat, rows),
        out_specs=(rows, rows, rows),
        check_vma=False,
    )
```

```python
import jax
import jax.numpy as jnp
from jax import lax
from jax.experimental import pallas as pl
from jax.experimental.pallas import tpu as pltpu
from jax.sharding import PartitionSpec as P

MESH = pl.DeviceIdType.MESH
F32 = jnp.float32
BF16 = jnp.bfloat16

D = 4096
Q = 48
HB = 128
W = 1024
HW = 512
HALF = D // 2
N = 8
HOPS = N // 2
FACTOR = D ** (-0.5)
NEG = -1e30
VMEM_LIMIT = 40 * 1024 * 1024


def nt(a, b):
    return lax.dot_general(a, b, (((1,), (1,)), ((), ())), preferred_element_type=F32)


def nn(a, b):
    return lax.dot_general(a, b, (((1,), (0,)), ((), ())), preferred_element_type=F32)


def tn(a, b):
    return lax.dot_general(a, b, (((0,), (0,)), ((), ())), preferred_element_type=F32)


def slot_of(rel):
    rel = rel % N
    return 0 if rel == 0 else (2 * rel - 1 if rel <= HOPS else 2 * (N - rel))


def rel_of(slot):
    return (slot + 1) // 2 if slot % 2 else (N - slot // 2) % N


SUM_PIECES = (6, 4, 2, 0)


def loop(n, body):
    for i in range(n):
        body(i)


def cols(i, size):
    return pl.ds(i * size, size)


def kernel(
    q_ref, p_ref, pool_ref, pos_ref, w_ref, req_ref,
    gq_ref, gp_ref, gpool_ref,
    q_all, pool2, ga, gb, meta, sc, pb, part, rx, st_out, st, ls, p_in, pos_in, w_in, req_in,
    q4, tin, cin, gpa, gpb, ra, rb, sa, sb, sa_in, sb_in,
    gq_acc, cb, gpo_out, gpo_in, gpo_acc,
    loc, qs, qr, ps, pr, ms, mr, a1s, a1r, b1s, b1r, ags, agr, sts, str_, lss, lsr,
    pts, ptr, gps, gpr, rss, rsr, a2s, a2r, b2s, b2r,
):
    g = lax.axis_index("group")
    mem = lax.axis_index("member")
    x, c = lax.div(g, 2), lax.rem(g, 2)
    y, z = lax.div(mem, N), lax.rem(mem, N)
    right = (lax.rem(x + 1, 4) * 2 + c, mem)
    left = (lax.rem(x + 3, 4) * 2 + c, mem)
    opp = (lax.rem(x + 2, 4) * 2 + c, mem)
    mate_group = x * 2 + 1 - c
    mate = (mate_group, mem)

    def yd(d):
        return (g, lax.rem(y + d, N) * N + z)

    def zd(d):
        return (g, y * N + lax.rem(z + d, N))

    def rc(src, dst, ssem, rsem, dev):
        return pltpu.make_async_remote_copy(
            src_ref=src, dst_ref=dst, send_sem=ssem, recv_sem=rsem,
            device_id=dev, device_id_type=MESH,
        )

    sent = []

    def go(copy):
        copy.start()
        sent.append(copy)

    waited = set()

    def arrived(ref, sem, key=None):
        if key is not None:
            if key in waited:
                return
            waited.add(key)
        rc(ref, ref, sem, sem, right).wait_recv()

    def all_sent(copies):
        for copy in copies:
            copy.wait_send()

    load_p = pltpu.make_async_copy(p_ref, p_in, loc.at[5])
    load_p.start()
    load_req = pltpu.make_async_copy(req_ref, req_in, loc.at[2])
    load_pos = pltpu.make_async_copy(pos_ref, pos_in, loc.at[3])
    load_w = pltpu.make_async_copy(w_ref, w_in, loc.at[4])
    load_req.start()
    load_pos.start()
    load_w.start()
    barrier = pltpu.get_barrier_semaphore()
    for dev in (right, left, opp, mate):
        pl.semaphore_signal(barrier, inc=1, device_id=dev, device_id_type=MESH)
    for d in range(1, N):
        pl.semaphore_signal(barrier, inc=1, device_id=yd(d), device_id_type=MESH)
        pl.semaphore_signal(barrier, inc=1, device_id=zd(d), device_id_type=MESH)

    load_q = pltpu.make_async_copy(q_ref, q_all.at[0], loc.at[0])
    load_pool = pltpu.make_async_copy(pool_ref, pool2.at[pl.ds(0, HB)], loc.at[1])
    load_q.start()
    load_pool.start()

    load_p.wait()
    pf = p_in[...].astype(F32)
    row16 = lax.broadcasted_iota(jnp.int32, (16, HW), 0)

    def fold(off):
        acc = jnp.zeros((16, HW), F32)
        for r in range(4):
            for k in range(4):
                piece = pf[r:r + 1, k * W + off:k * W + off + HW]
                acc = jnp.where(row16 == 4 * r + k, piece, acc)
        return acc.astype(BF16)

    ga[0, 0] = fold(0)
    gb[0, 0] = fold(HW)
    meta[0] = jnp.zeros((8, 128), F32)
    load_req.wait()
    load_pos.wait()
    load_w.wait()
    meta[0, 0:1, 0:8] = req_in[...].astype(F32)

    pl.semaphore_wait(barrier, 4 + 2 * (N - 1))

    for d in (4, 3, 5, 2, 6, 1, 7):
        go(rc(ga.at[0, 0], ga.at[0, slot_of(d)], a1s.at[d], a1r.at[d], zd(d)))
        go(rc(gb.at[0, 0], gb.at[slot_of(d), 0], b1s.at[d], b1r.at[d], yd(d)))
    h0, h1 = pl.ds(0, HALF), pl.ds(HALF, HALF)
    go(rc(q_ref.at[:, h0], q_all.at[1, :, h0], qs.at[0], qr.at[0], right))
    go(rc(q_ref.at[:, h1], q_all.at[2, :, h1], qs.at[1], qr.at[1], left))
    go(rc(meta.at[0], meta.at[1], ms.at[0], mr.at[0], right))
    go(rc(meta.at[0], meta.at[2], ms.at[1], mr.at[1], left))
    go(rc(meta.at[0], meta.at[3], ms.at[2], mr.at[2], opp))
    go(rc(pool_ref, pool2.at[pl.ds(HB, HB)], ps.at[0], pr.at[0], mate))
    go(rc(q_ref.at[:, h1], q_all.at[1, :, h1], qs.at[2], qr.at[2], right))
    go(rc(q_ref.at[:, h0], q_all.at[2, :, h0], qs.at[3], qr.at[3], left))

    def ring_view(flow, rel, part):
        near = pl.ds(4 * part, 4)
        return ga.at[slot_of(rel), near] if flow < 2 else gb.at[near, slot_of(rel)]

    def ring_go(flow, src_rel, dst_rel, hops, step, part):
        hop = N - hops if flow % 2 else hops
        sem = 2 * step + part
        go(rc(
            ring_view(flow, src_rel, part), ring_view(flow, dst_rel, part),
            ags.at[flow, sem], agr.at[flow, sem], yd(hop) if flow < 2 else zd(hop),
        ))

    def ring_arrived(flow, step, part):
        rel = (step + 1) * (1 if flow % 2 == 0 else -1)
        arrived(ring_view(flow, rel, part), agr.at[flow, 2 * step + part], ("ring", flow, step, part))

    def ring_step(step, part):
        for flow in range(4):
            sign = 1 if flow % 2 == 0 else -1
            if step == 0:
                for slot in range(max(4 * part, 1), 4 * part + 4):
                    rel = rel_of(slot)
                    if flow < 2:
                        arrived(ga.at[0, slot], a1r.at[rel], ("a1", rel))
                    else:
                        arrived(gb.at[slot, 0], b1r.at[rel], ("b1", rel))
            else:
                ring_arrived(flow, step - 1, part)
            ring_go(flow, sign * step, sign * (step + 1), 1, step, part)
            if step == 2 and flow % 2 == part:
                ring_go(flow, sign * 2, 4, 2, 3, part)

    ring_step(0, 0)
    ring_step(0, 1)

    lane256 = lax.broadcasted_iota(jnp.int32, (1, 2 * HB), 1)
    lane128 = lax.broadcasted_iota(jnp.int32, (1, 128), 1)

    row8 = lax.broadcasted_iota(jnp.int32, (8, 1), 0)
    diagonal = lax.broadcasted_iota(jnp.int32, (Q, 1), 0) == lane128

    def as_row(column):
        return jnp.sum(jnp.where(diagonal, column, 0.0), axis=0, keepdims=True)

    def as_column(row):
        return jnp.sum(jnp.where(diagonal, row, 0.0), axis=1, keepdims=True)

    def hard(slot):
        scores = nt(q_all[slot], pool2[...]) * FACTOR
        line = meta[slot, 0:1, :]
        here = jnp.sum(jnp.where(lane128 == g, line, 0.0), axis=1, keepdims=True)
        there = jnp.sum(jnp.where(lane128 == mate_group, line, 0.0), axis=1, keepdims=True)
        asked = jnp.where(lane256 < HB, here, there) != 0.0
        scores = jnp.where(asked, scores, NEG)
        sc[slot] = scores
        top = jnp.max(scores, axis=1, keepdims=True)
        probs = jnp.where(asked, jnp.exp(scores - top), 0.0)
        total = jnp.sum(probs, axis=1, keepdims=True)
        pb[slot] = probs.astype(BF16)
        st_out[slot] = jnp.where(row8 == 0, as_row(top), as_row(total))

    def partial(slot, dest, theirs):
        for half in (0, 1):
            def body(i):
                at = cols(i + 4 * half, 512)
                part[slot, :, at] = nn(pb[slot], pool2[:, at]).astype(BF16)

            loop(4, body)
            at, sem = pl.ds(half * HALF, HALF), 2 * theirs + half
            go(rc(part.at[slot, :, at], rx.at[theirs, :, at], pts.at[sem], ptr.at[sem], dest))

    load_q.wait()
    load_pool.wait()
    arrived(pool2.at[pl.ds(HB, HB)], pr.at[0])
    hard(0)
    for k in range(4):
        q4[k * Q:(k + 1) * Q, :] = q_all[0, :, k * W:(k + 1) * W]
    arrived(q_all.at[1, :, h0], qr.at[0])
    go(rc(q_all.at[1, :, h0], q_all.at[3, :, h0], qs.at[4], qr.at[4], right))
    arrived(q_all.at[2, :, h1], qr.at[1])
    go(rc(q_all.at[2, :, h1], q_all.at[3, :, h1], qs.at[5], qr.at[5], left))
    for step in (1, 2):
        ring_step(step, 0)
        ring_step(step, 1)

    arrived(q_all.at[1, :, h1], qr.at[2])
    arrived(meta.at[1], mr.at[0])
    hard(1)
    go(rc(st_out.at[1], st.at[2], sts.at[0], str_.at[0], left))
    arrived(q_all.at[2, :, h0], qr.at[3])
    arrived(meta.at[2], mr.at[1])
    hard(2)
    go(rc(st_out.at[2], st.at[1], sts.at[1], str_.at[1], right))

    arrived(q_all.at[3, :, h0], qr.at[4])
    arrived(q_all.at[3, :, h1], qr.at[5])
    arrived(meta.at[3], mr.at[2])
    hard(3)
    go(rc(st_out.at[3], st.at[3], sts.at[2], str_.at[2], opp))
    early = list(sent)
    sent.clear()

    for flow in range(4):
        for half in (0, 1):
            ring_arrived(flow, 2, half)
        ring_arrived(flow, 3, flow % 2)
    mod4 = lax.rem(lane256, 4)

    def in_block(b):
        pa = ga[pl.ds(2 * b, 2)].reshape(256, HW)
        pbk = gb[pl.ds(2 * b, 2)].reshape(256, HW)
        s = nt(q4[:, 0:HW], pa) + nt(q4[:, HW:W], pbk)
        t = jnp.where(mod4 == 0, s[0:Q], 0.0)
        for k in range(1, 4):
            t = jnp.where(mod4 == k, s[k * Q:(k + 1) * Q], t)
        t = t + jnp.where(lax.rem(mod4, 2) == 0, pltpu.roll(t, 255, 1), pltpu.roll(t, 1, 1))
        t = t + jnp.where(mod4 < 2, pltpu.roll(t, 254, 1), pltpu.roll(t, 2, 1))
        tin[:, cols(b, 256)] = t * FACTOR

    loop(4, in_block)

    for i in range(3):
        arrived(st.at[(2, 1, 3)[i]], str_.at[i])
    found = [st_out[0]] + [st[i] for i in (1, 2, 3)]
    tops = [as_column(f[0:1]) for f in found]
    sums = [as_column(f[1:2]) for f in found]
    t_in = tin[...]
    highest = jnp.max(t_in, axis=1, keepdims=True)
    for t in tops:
        highest = jnp.maximum(highest, t)
    lane1024 = lax.broadcasted_iota(jnp.int32, (1, W), 1)
    quarter = lax.rem(lane1024, 4)
    totals = jnp.sum(
        jnp.where(quarter == 0, jnp.exp(t_in - highest), 0.0), axis=1, keepdims=True
    )
    for t, s in zip(tops, sums):
        totals = totals + s * jnp.exp(t - highest)
    logsum = highest + jnp.log(totals)
    eye = lax.broadcasted_iota(jnp.int32, (Q, Q), 0) == lax.broadcasted_iota(jnp.int32, (Q, Q), 1)
    weight = jnp.sum(jnp.where(eye, w_in[...], 0.0), axis=1, keepdims=True)
    positive = jnp.sum(jnp.where(eye, pos_in[...], 0), axis=1, keepdims=True)
    ls[0] = jnp.where(lane128 < 64, logsum, weight)
    go(rc(ls.at[0], ls.at[1], lss.at[0], lsr.at[0], right))
    go(rc(ls.at[0], ls.at[2], lss.at[1], lsr.at[1], left))
    go(rc(ls.at[0], ls.at[3], lss.at[2], lsr.at[2], opp))

    def rel_at(slot):
        half = lax.div(slot + 1, 2)
        return jnp.where(lax.rem(slot, 2) == 1, half, lax.rem(N - half, N))

    from_y = lax.rem(y + N - rel_at(lax.div(lane1024, 128)), N)
    from_z = lax.rem(z + N - rel_at(lax.rem(lax.div(lane1024, 16), N)), N)
    passage = (from_y * N + from_z) * 4 + lax.rem(lax.div(lane1024, 4), 4)
    one_hot = (passage == positive).astype(F32)
    coefs = weight * (jnp.exp(t_in - logsum) - one_hot) * FACTOR
    for k in range(4):
        cin[k * Q:(k + 1) * Q, :] = jnp.where(quarter == k, coefs, 0.0).astype(BF16)

    def gp_block(b):
        rows = tn(cin[:, cols(b, 128)], q4[...]).astype(BF16)
        gpa[b] = rows[:, 0:HW].reshape(N, 16, HW)
        gpb[b] = rows[:, HW:W].reshape(N, 16, HW)

    def sum_view(flow, d, u):
        slot = slot_of(N - d if flow % 2 == 0 else d)
        pair = pl.ds(SUM_PIECES[u], 2)
        return gpa.at[pair, slot] if flow < 2 else gpb.at[slot, pair]

    def sum_slot(flow, kind, u):
        return (ra if flow < 2 else rb).at[flow % 2, kind, pl.ds(SUM_PIECES[u], 2)]

    def sum_go(flow, d, kind, hops, u):
        hop = hops if flow % 2 == 0 else N - hops
        sem = kind * 4 + u
        go(rc(
            sum_view(flow, d, u), sum_slot(flow, kind, u), rss.at[flow, sem], rsr.at[flow, sem],
            zd(hop) if flow < 2 else yd(hop),
        ))

    def sum_add(flow, d, kind, u):
        arrived(sum_slot(flow, kind, u), rsr.at[flow, kind * 4 + u])
        view = sum_view(flow, d, u)
        view[...] = view[...] + sum_slot(flow, kind, u)[...]

    def from_four(flow, u):
        return (u < 2) == (flow % 2 == 0)

    def sum_first(flows):
        for u in range(4):
            for flow in flows:
                if from_four(flow, u):
                    sum_go(flow, 4, 1, 2, u)
                sum_go(flow, 3, 0, 1, u)

    def sum_second():
        for u in range(4):
            for flow in range(4):
                sum_add(flow, 2, 0, u)
                if from_four(flow, u):
                    sum_add(flow, 2, 1, u)
                sum_go(flow, 2, 2, 1, u)

    def sum_third():
        for u in range(4):
            for flow in range(4):
                sum_add(flow, 1, 2, u)
                sum_go(flow, 1, 3, 1, u)

    loop(3, lambda i: gp_block(N - 1 - i))
    sum_first((2, 3))
    loop(N - 3, gp_block)
    sum_first((0, 1))

    partial(1, left, 1)
    partial(2, right, 0)
    partial(3, opp, 2)

    def coef_rows(slot):
        lsum, wt = ls[slot][:, 0:1], ls[slot][:, 64:65]
        cb[slot * Q:(slot + 1) * Q, :] = (wt * jnp.exp(sc[slot] - lsum) * FACTOR).astype(BF16)

    coef_rows(0)

    def own_rows(i):
        at = cols(i, 512)
        gq_acc[:, at] = nn(cb[0:Q, :], pool2[:, at])

    loop(8, own_rows)

    sum_second()

    for h, ref in ((0, ga), (1, gb)):
        for n in range(2):
            rows = nn(cin[...], ref[:, :, :, n * 256:(n + 1) * 256].reshape(W, 256))
            for k in range(4):
                to = pl.ds(k * W + h * HW + n * 256, 256)
                gq_acc[:, to] = gq_acc[:, to] + rows[k * Q:(k + 1) * Q]

    later = list(sent)
    sent.clear()
    sum_third()
    all_sent(early)

    for i in range(3):
        arrived(ls.at[i + 1], lsr.at[i])
        coef_rows(i + 1)

    def far_pool(i):
        at = cols(i, 512)
        gpo_out[:, at] = tn(cb[:, HB:2 * HB], q_all[:, :, at].reshape(4 * Q, 512)).astype(BF16)

    loop(8, far_pool)
    go(rc(gpo_out, gpo_in, gps.at[0], gpr.at[0], mate))

    def near_pool(i):
        at = cols(i, 512)
        gpo_acc[:, at] = tn(cb[:, 0:HB], q_all[:, :, at].reshape(4 * Q, 512))

    for u in range(4):
        for flow in range(4):
            arrived(sum_slot(flow, 3, u), rsr.at[flow, 12 + u])
        first = SUM_PIECES[u]
        pair = pl.ds(first, 2)
        sa[pair] = (
            gpa[pair, 0].astype(F32) + ra[0, 3, pair].astype(F32)
            + ra[1, 3, pair].astype(F32)
        ).astype(BF16)
        sb[pair] = (
            gpb[0, pair].astype(F32) + rb[0, 3, pair].astype(F32)
            + rb[1, 3, pair].astype(F32)
        ).astype(BF16)
        for slot in (first + 1, first):
            if slot > 0:
                d = N - rel_of(slot)
                go(rc(sa.at[slot], sa_in.at[slot], a2s.at[slot], a2r.at[slot], yd(d)))
                go(rc(sb.at[slot], sb_in.at[slot], b2s.at[slot], b2r.at[slot], zd(d)))

    loop(8, near_pool)
    all_sent(later)
    arrived(gpo_in, gpr.at[0])

    def pool_sum(i):
        at = cols(i, 512)
        gpool_ref[:, at] = (gpo_acc[:, at] + gpo_in[:, at].astype(F32)).astype(BF16)

    loop(8, pool_sum)

    scales = [weight * FACTOR * jnp.exp(t - logsum) for t in tops[1:]]
    for half in (0, 1):
        for way in range(3):
            arrived(rx.at[way, :, pl.ds(half * HALF, HALF)], ptr.at[2 * way + half])

    def finish(i):
        at = cols(i, 512)
        acc = gq_acc[:, at]
        for way in range(3):
            acc = acc + rx[way, :, at].astype(F32) * scales[way]
        gq_ref[:, at] = acc.astype(BF16)

    loop(8, finish)

    row4 = lax.broadcasted_iota(jnp.int32, (4, HW), 0)
    for h, own, held, sem in ((0, sa[0], sa_in, a2r), (1, sb[0], sb_in, b2r)):
        acc = own.astype(F32)
        for slot in range(1, N):
            arrived(held.at[slot], sem.at[slot])
            acc = acc + held[slot].astype(F32)
        for k in range(4):
            out = jnp.zeros((4, HW), F32)
            for r in range(4):
                out = jnp.where(row4 == r, acc[4 * r + k:4 * r + k + 1, :], out)
            gp_ref[:, k * W + h * HW:k * W + (h + 1) * HW] = out.astype(BF16)

    all_sent(sent)


def store(q_in, p_in, pool_in, q_out, p_out, pool_out, sem):
    pairs = ((pool_in, pool_out), (q_in, q_out), (p_in, p_out))
    copies = [pltpu.make_async_copy(src, dst, sem.at[i]) for i, (src, dst) in enumerate(pairs)]
    for copy in copies:
        copy.start()
    for copy in copies:
        copy.wait()


def per_device(queries, passages, pool, positives, weights, requests):
    dma = pltpu.SemaphoreType.DMA
    v = pltpu.VMEM
    scratch = [
        v((4, Q, D), BF16),
        v((2 * HB, D), BF16),
        v((N, N, 16, HW), BF16),
        v((N, N, 16, HW), BF16),
        v((4, 8, 128), F32),
        v((4, Q, 2 * HB), F32),
        v((4, Q, 2 * HB), BF16),
        v((4, Q, D), BF16),
        v((3, Q, D), BF16),
        v((4, 8, 128), F32),
        v((4, 8, 128), F32),
        v((4, Q, 128), F32),
        v((4, D), BF16),
        v((1, Q), jnp.int32),
        v((1, Q), F32),
        v((1, 8), jnp.int32),
        v((4 * Q, W), BF16),
        v((Q, W), F32),
        v((4 * Q, W), BF16),
        v((N, N, 16, HW), BF16),
        v((N, N, 16, HW), BF16),
        v((2, 4, N, 16, HW), BF16),
        v((2, 4, N, 16, HW), BF16),
        v((N, 16, HW), BF16),
        v((N, 16, HW), BF16),
        v((N, 16, HW), BF16),
        v((N, 16, HW), BF16),
        v((Q, D), F32),
        v((4 * Q, 2 * HB), BF16),
        v((HB, D), BF16),
        v((HB, D), BF16),
        v((HB, D), F32),
        dma((6,)),
        dma((6,)), dma((6,)),
        dma((1,)), dma((1,)),
        dma((3,)), dma((3,)),
        dma((N,)), dma((N,)), dma((N,)), dma((N,)),
        dma((4, 8)), dma((4, 8)),
        dma((3,)), dma((3,)),
        dma((3,)), dma((3,)),
        dma((6,)), dma((6,)),
        dma((1,)), dma((1,)),
        dma((4, 16)), dma((4, 16)),
        dma((N,)), dma((N,)), dma((N,)), dma((N,)),
    ]
    hbm = pl.BlockSpec(memory_space=pltpu.HBM)
    vmem = pl.BlockSpec(memory_space=pltpu.VMEM)
    outs = pl.pallas_call(
        kernel,
        out_shape=(
            jax.ShapeDtypeStruct((Q, D), BF16),
            jax.ShapeDtypeStruct((4, D), BF16),
            jax.ShapeDtypeStruct((HB, D), BF16),
        ),
        in_specs=[hbm] * 6,
        out_specs=(vmem,) * 3,
        scratch_shapes=scratch,
        compiler_params=pltpu.CompilerParams(
            collective_id=0, has_side_effects=True, vmem_limit_bytes=VMEM_LIMIT
        ),
        cost_estimate=pl.CostEstimate(flops=2_500_000_000, bytes_accessed=3_000_000, transcendentals=200_000),
    )(*(
        pltpu.with_memory_space_constraint(a, pltpu.HBM)
        for a in (queries, passages, pool, positives.reshape(1, Q), weights.reshape(1, Q), requests)
    ))
    return pl.pallas_call(
        store,
        out_shape=tuple(jax.ShapeDtypeStruct(o.shape, o.dtype) for o in outs),
        in_specs=[vmem] * 3,
        out_specs=(pl.BlockSpec(memory_space=pl.ANY),) * 3,
        scratch_shapes=[dma((3,))],
        compiler_params=pltpu.CompilerParams(vmem_limit_bytes=1024 * 1024),
    )(*outs)


def solution(mesh):
    rows = P(("group", "member"), None)
    flat = P(("group", "member"))
    return jax.shard_map(
        per_device,
        mesh=mesh,
        in_specs=(rows, rows, rows, flat, flat, rows),
        out_specs=(rows, rows, rows),
        check_vma=False,
    )
```
